512 devices in a mesh: inp: 128 (over y, z, core), sec: 4 (over x).
Axes of the slice: x: 4, y: 8, z: 8, core: 2. Of those that a mesh axis runs over, the one named last changes fastest.
Arguments:
- voltages: bfloat16 [2, 2048, 32768], P(None, 'inp', 'sec'), may hold values from -6 to 6
- filter_taps: float32 [4, 1024], replicated, may hold values from -3 to 3
- flagged: int32 [64], replicated, may hold values from 0 to 1023, as said below
- channel_owner: int32 [1024], replicated, may hold values from 0 to 127, as said below
- ref_inputs: int32 [12], replicated, may hold values from 0 to 2047, as said below
Outputs:
- visibilities: float32 [128, 16, 2, 12, 2048], P('inp', None, None, None, 'sec')
The draws below stay inside these ranges and needn't reach their ends.
Inputs may be any that keep to these rules, and one draw needn't show every extreme that they name: `flagged`: 64 distinct channels. `channel_owner`: no owner has more than 16 channels in all; some owner has exactly 16 unflagged channels. `ref_inputs`: 12 distinct inputs, among them input 0 and input 2048 - 1.
All inputs are finite; a program needn't handle non-finite values.
Results may differ from the reference program's by a relative error of at most 0.004.
Values may be sent and summed in bfloat16 or wider, within the bound.
A program may use at most 64 MiB of HBM per device.

```python
import jax
import jax.numpy as jnp
from jax import lax

IN_DEV = 16
CHANNELS = 1024
TAPS = 4
REFS = 12
NFLAG = 64
INPUTS = 2048
OWNERS = 128
CAP = 16
SLOTS = 2048
BLOCKS = 32
SAMPLES = 32768
N_INP = 128


def layout(key):
    channel_order = jax.random.permutation(jax.random.fold_in(key, 101), CHANNELS)
    slot_order = jax.random.permutation(jax.random.fold_in(key, 102), SLOTS)
    full_owner = jax.random.randint(jax.random.fold_in(key, 103), (), 0, OWNERS)
    leading = jnp.where(slot_order // CAP == full_owner, 0, 1).astype(jnp.int32)
    ranked = jnp.argsort(leading, stable=True)
    chosen = slot_order[ranked][:CHANNELS]
    owners_drawn = jnp.zeros((CHANNELS,), jnp.int32).at[channel_order].set((chosen // CAP).astype(jnp.int32))
    flagged_drawn = channel_order[CHANNELS - NFLAG:].astype(jnp.int32)
    return (owners_drawn, flagged_drawn)


def draw_flagged(key, part):
    shared = layout(key)
    return shared[1]


def draw_channel_owner(key, part):
    shared = layout(key)
    return shared[0]


def draw_ref_inputs(key, part):
    key = jax.random.fold_in(key, 3)
    middle = jax.random.permutation(jax.random.fold_in(key, 1), INPUTS - 2)[:REFS - 2] + 1
    ends = jnp.array([0, INPUTS - 1], jnp.int32)
    listed = jnp.concatenate([ends, middle.astype(jnp.int32)])
    shuffle = jax.random.permutation(jax.random.fold_in(key, 2), REFS)
    return listed[shuffle].astype(jnp.int32)


def levels(stream_key, extent, pieces, least, largest):
    level, own = 1.0, jax.random.fold_in(stream_key, 6)
    for position, shards_of in pieces:
        heights = jnp.exp(jax.random.uniform(jax.random.fold_in(own, position), (shards_of,), jnp.float32, least / len(pieces), largest / len(pieces)))
        level = level * jnp.repeat(heights, extent[position] // shards_of).reshape([-1 if axis == position else 1 for axis in range(len(extent))])
    return level


def scatter_about(own_key, extent, deviation, bound, cuts=(), kind=jnp.bfloat16):
    loudness = levels(own_key, extent, cuts, -0.22, 0.18) if cuts else 1.0
    entries = jax.random.normal(own_key, extent, jnp.float32) * deviation * loudness
    return jnp.minimum(jnp.maximum(entries, -bound), bound).astype(kind)


def setup_inputs(seed: int = 0) -> dict:
    keys = jax.random.split(jax.random.key(seed), 6)
    voltages = scatter_about(keys[0], (2, INPUTS, SAMPLES), 1.0, 6.0, ((1, 128), (2, 4)))
    filter_taps = scatter_about(keys[1], (TAPS, CHANNELS), 0.5, 3.0, (), jnp.float32)
    flagged = draw_flagged(jax.random.fold_in(keys[5], 71), 0)
    channel_owner = draw_channel_owner(jax.random.fold_in(keys[5], 71), 0)
    ref_inputs = draw_ref_inputs(jax.random.fold_in(keys[5], 71), 0)
    return dict(voltages=voltages, filter_taps=filter_taps, flagged=flagged, channel_owner=channel_owner, ref_inputs=ref_inputs)


def slot_table(flagged, channel_owner, owners, capacity):
    channel_count = channel_owner.shape[0]
    channel_ids = jnp.arange(channel_count, dtype=jnp.int32)
    dropped = jnp.any(channel_ids[:, None] == flagged[None, :], axis=1)
    member = ((channel_owner[:, None] == jnp.arange(owners, dtype=jnp.int32)[None, :]) & (~dropped)[:, None]).astype(jnp.int32)
    before = (jnp.cumsum(member, axis=0) - member).astype(jnp.int32)
    slot_rank = lax.optimization_barrier(jnp.sum(before * member, axis=1)).astype(jnp.int32)
    target = jnp.where(dropped, owners * capacity, channel_owner * capacity + slot_rank).astype(jnp.int32)
    table = jnp.full((owners * capacity + 1,), -1, jnp.int32).at[target].set(channel_ids)
    return table[:owners * capacity]

def reference(voltages, filter_taps, flagged, channel_owner, ref_inputs):
    slot_channel = slot_table(flagged, channel_owner, N_INP, CAP)
    grouped = voltages.reshape(2, N_INP, IN_DEV, BLOCKS, CHANNELS).transpose(1, 0, 2, 3, 4)

    def spectra_of(group):
        frames = group.astype(jnp.float32)
        padded = jnp.concatenate([frames, jnp.zeros((2, IN_DEV, TAPS - 1, CHANNELS), jnp.float32)], axis=2)
        filtered = jnp.zeros_like(frames)
        for tap_index in range(TAPS):
            filtered = filtered + filter_taps[tap_index] * padded[:, :, tap_index:tap_index + BLOCKS]
        transformed = jnp.fft.fft(lax.complex(filtered[0], filtered[1]), axis=-1) / jnp.sqrt(float(CHANNELS))
        return jnp.stack([jnp.real(transformed), jnp.imag(transformed)]).astype(jnp.bfloat16)
    spectra = lax.map(spectra_of, grouped)
    spectra = spectra.transpose(1, 3, 0, 2, 4).reshape(2, BLOCKS, INPUTS, CHANNELS)

    def owner_vis(owner_index):
        chosen = lax.dynamic_slice_in_dim(slot_channel, owner_index * CAP, CAP)
        picked = jnp.take(spectra, jnp.maximum(chosen, 0), axis=3).astype(jnp.float32)
        ref_part = jnp.take(picked, ref_inputs, axis=2)
        real_vis = jnp.einsum('pbic,pbrc->cri', picked, ref_part)
        imag_vis = jnp.einsum('bic,brc->cri', picked[1], ref_part[0]) - jnp.einsum('bic,brc->cri', picked[0], ref_part[1])
        stacked = jnp.stack([real_vis, imag_vis], axis=1) / BLOCKS
        return stacked * (chosen >= 0).astype(jnp.float32)[:, None, None, None]
    return lax.map(owner_vis, jnp.arange(N_INP, dtype=jnp.int32))
```

```python
import functools
import math

import jax
import jax.numpy as jnp
import numpy as np
from jax import lax
from jax.experimental import pallas as pl
from jax.experimental.pallas import tpu as pltpu
from jax.sharding import PartitionSpec as P

CHANNELS = 1024
TAPS = 4
RADIX = 4
SHORT = CHANNELS // RADIX
CAPACITY = 16
LOCAL = 16
HALF = 4
LANES = 128
GROUP = LANES // CAPACITY
REF_ROWS = 16
MESH = pl.DeviceIdType.MESH


def tables():
    n = np.arange(SHORT)
    angle = 2.0 * math.pi * ((n[:, None] * n[None, :]) % SHORT) / SHORT
    cos, sin = np.cos(angle), np.sin(angle)
    full = np.block([[cos, -sin], [sin, cos]]) / math.sqrt(CHANNELS)
    high = full.astype(np.float32).astype(jnp.bfloat16)
    low = (full - high.astype(np.float64)).astype(np.float32).astype(jnp.bfloat16)
    turn = 2.0 * math.pi * np.arange(RADIX)[:, None] * n[None, :] / CHANNELS
    twiddle = np.stack([np.cos(turn), np.sin(turn)], axis=1).reshape(2 * RADIX, SHORT)
    return high, low, twiddle.astype(np.float32)


def kernel(owners, sections, volt, taps, target, refs, high, low, twiddle, out,
           halo, zhi, zlo, stage, onehot, outbox, inbox, refbox, refin, weights,
           halo_sem, send_sem, recv_sem, ref_send, ref_recv):
    p, s = lax.axis_index("inp"), lax.axis_index("sec")
    span = owners // sections
    q = lax.div(p, span)
    place = lax.rem(p, span)
    own_group = lax.div(p, GROUP)
    groups = owners // GROUP
    rows = span * LOCAL
    at_home = q == s

    barrier = pltpu.get_barrier_semaphore()

    def greet(k, carry):
        there_p = s * span + lax.rem(k, span)
        there_s = lax.div(k, span)

        @pl.when(jnp.logical_not((there_p == p) & (there_s == s)))
        def _():
            pl.semaphore_signal(barrier, inc=1, device_id=(there_p, there_s), device_id_type=MESH)
        return carry
    lax.fori_loop(0, owners, greet, 0)
    for d in range(1, sections):
        pl.semaphore_signal(barrier, inc=1, device_id=(p, lax.rem(s + d, sections)), device_id_type=MESH)

    lane = lax.broadcasted_iota(jnp.int32, (LOCAL, LANES), 1)
    block = lane // CAPACITY

    def spectra(h):
        for b in range(HALF):
            parts = []
            for part in range(2):
                pieces = []
                for n1 in range(RADIX):
                    total = None
                    for t in range(TAPS):
                        frame = h * HALF + b + t
                        if frame < 2 * HALF:
                            source = volt[part, :, pl.ds(frame * CHANNELS + n1 * SHORT, SHORT)].astype(jnp.float32)
                        else:
                            source = halo[part, :, pl.ds((frame - 2 * HALF) * CHANNELS + n1 * SHORT, SHORT)].astype(jnp.float32)
                            source = jnp.where(s == sections - 1, 0.0, source)
                        term = taps[t:t + 1, n1 * SHORT:(n1 + 1) * SHORT] * source
                        total = term if total is None else total + term
                    pieces.append(total)
                parts.append(pieces)
            (r0, r1, r2, r3), (i0, i1, i2, i3) = parts
            ar, ai, br, bi = r0 + r2, i0 + i2, r0 - r2, i0 - i2
            cr, ci, dr, di = r1 + r3, i1 + i3, r1 - r3, i1 - i3
            mixed = [(ar + cr, ai + ci), (br + di, bi - dr), (ar - cr, ai - ci), (br - di, bi + dr)]
            for c1 in range(RADIX):
                re, im = mixed[c1]
                if c1:
                    cos, sin = twiddle[2 * c1:2 * c1 + 1, :], twiddle[2 * c1 + 1:2 * c1 + 2, :]
                    re, im = re * cos + im * sin, im * cos - re * sin
                at = pl.ds((c1 * HALF + b) * LOCAL, LOCAL)
                for k, value in enumerate((re, im)):
                    top = value.astype(jnp.bfloat16)
                    zhi[at, k * SHORT:(k + 1) * SHORT] = top
                    zlo[at, k * SHORT:(k + 1) * SHORT] = (value - top.astype(jnp.float32)).astype(jnp.bfloat16)
        top = zhi[...]
        product = jnp.dot(top, high[...], preferred_element_type=jnp.float32)
        product += jnp.dot(zlo[...], high[...], preferred_element_type=jnp.float32)
        product += jnp.dot(top, low[...], preferred_element_type=jnp.float32)
        product = product.astype(jnp.bfloat16)
        deep = HALF * LOCAL
        for c1 in range(RADIX):
            for part in range(2):
                stage[h, part * deep:(part + 1) * deep, c1 * SHORT:(c1 + 1) * SHORT] = (
                    product[c1 * deep:(c1 + 1) * deep, part * SHORT:(part + 1) * SHORT])

    def build(j, carry):
        base = pl.multiple_of(j * LANES, LANES)
        slot = lax.broadcasted_iota(jnp.int32, (SHORT, LANES), 1) + j * LANES
        for c1 in range(RADIX):
            hit = target[:, c1:c1 + 1] == slot
            onehot[c1 * SHORT:(c1 + 1) * SHORT, pl.ds(base, LANES)] = jnp.where(hit, 1.0, 0.0).astype(jnp.bfloat16)
        return carry

    def ship(h):
        def one_group(j, carry):
            g = lax.rem(own_group + j, groups)
            base = pl.multiple_of(g * LANES, LANES)
            picked = jnp.dot(stage[h], onehot[:, pl.ds(base, LANES)], preferred_element_type=jnp.float32)
            tiles = []
            for k in range(GROUP):
                tile = picked[k * LOCAL:(k + 1) * LOCAL, :]
                tiles.append(pltpu.roll(tile, k * CAPACITY, 1) if k else tile)
            for bit in range(3):
                step = 1 << bit
                taken = ((block // step) % 2) == 1
                tiles = [jnp.where(taken, tiles[(m + step) % GROUP], tiles[m]) for m in range(GROUP)]
            for k in range(GROUP):
                outbox[h, g * GROUP + k] = tiles[(GROUP - k) % GROUP].astype(jnp.bfloat16)
            for k in range(GROUP):
                o = g * GROUP + k
                landing = inbox.at[h, s, pl.ds(pl.multiple_of(place * LOCAL, LOCAL), LOCAL), :]
                mine = (o == p) & at_home

                @pl.when(mine)
                def _():
                    pltpu.make_async_copy(outbox.at[h, o], landing, recv_sem.at[h]).start()

                @pl.when(jnp.logical_not(mine))
                def _():
                    pltpu.make_async_remote_copy(
                        src_ref=outbox.at[h, o], dst_ref=landing, send_sem=send_sem.at[h],
                        recv_sem=recv_sem.at[h], device_id=(o, q), device_id_type=MESH).start()
            return carry
        lax.fori_loop(0, groups, one_group, 0)

    lax.fori_loop(0, groups, build, 0)
    spectra(0)

    @pl.when(at_home)
    def _():
        pl.semaphore_wait(barrier, owners - 1 + sections - 1)

    @pl.when(jnp.logical_not(at_home))
    def _():
        pl.semaphore_wait(barrier, owners + sections - 1)

    halo_copy = pltpu.make_async_remote_copy(
        src_ref=volt.at[:, :, pl.ds(0, (TAPS - 1) * CHANNELS)], dst_ref=halo, send_sem=halo_sem.at[0],
        recv_sem=halo_sem.at[1], device_id=(p, lax.rem(s + sections - 1, sections)), device_id_type=MESH)
    halo_copy.start()
    ship(0)
    halo_copy.wait()
    spectra(1)
    ship(1)

    index = lax.broadcasted_iota(jnp.int32, (REF_ROWS, rows), 1) + s * rows
    chosen = jnp.where(refs[...] == index, 1.0, 0.0).astype(jnp.bfloat16)

    def gather_refs(h):
        pltpu.make_async_copy(inbox.at[h], inbox.at[h], recv_sem.at[h]).wait()
        for t in range(sections):
            found = jnp.dot(chosen, inbox[h, t], preferred_element_type=jnp.float32)
            refbox[h, t * REF_ROWS:(t + 1) * REF_ROWS, :] = found.astype(jnp.bfloat16)
        copies = []
        for d in range(1, sections):
            copies.append(pltpu.make_async_remote_copy(
                src_ref=refbox.at[h], dst_ref=refin.at[h, d - 1], send_sem=ref_send.at[h, d - 1],
                recv_sem=ref_recv.at[h, d - 1], device_id=(p, lax.rem(s + d, sections)), device_id_type=MESH))
        for copy in copies:
            copy.start()
        return copies

    wide = lax.broadcasted_iota(jnp.int32, (REF_ROWS, LANES), 1)
    inner = wide % CAPACITY
    part_of = ((wide // CAPACITY + (GROUP - lax.rem(p, GROUP))) % GROUP) // HALF
    sign = jnp.where(part_of == 1, 1.0, -1.0)

    def correlate(h, copies):
        for copy in copies:
            copy.wait()
        total = None
        for t in range(sections):
            at = pl.ds(t * REF_ROWS, REF_ROWS)
            found = refbox[h, at, :].astype(jnp.float32)
            for d in range(1, sections):
                found += refin[h, d - 1, at, :].astype(jnp.float32)
            turned = pltpu.roll(found, LANES // 2, 1) * sign
            for k in range(CAPACITY):
                keep = inner == k
                weights[2 * k * REF_ROWS:(2 * k + 1) * REF_ROWS, t * LANES:(t + 1) * LANES] = (
                    jnp.where(keep, found, 0.0).astype(jnp.bfloat16))
                weights[(2 * k + 1) * REF_ROWS:(2 * k + 2) * REF_ROWS, t * LANES:(t + 1) * LANES] = (
                    jnp.where(keep, turned, 0.0).astype(jnp.bfloat16))
            term = lax.dot_general(weights[:, t * LANES:(t + 1) * LANES], inbox[h, t],
                                   (((1,), (1,)), ((), ())), preferred_element_type=jnp.float32)
            total = term if total is None else total + term
        return total

    first = gather_refs(0)
    total = correlate(0, first)
    second = gather_refs(1)
    total = total + correlate(1, second)
    total = total * (1.0 / (2 * HALF * sections))
    width = out.shape[3]
    for k in range(CAPACITY):
        for part in range(2):
            at = (2 * k + part) * REF_ROWS
            out[0, k, part] = total[at:at + width, :]

    for h in range(2):
        @pl.when(at_home)
        def _():
            some = outbox.at[h, pl.ds(0, owners - 1)]
            pltpu.make_async_copy(some, some, send_sem.at[h]).wait()

        @pl.when(jnp.logical_not(at_home))
        def _():
            pltpu.make_async_copy(outbox.at[h], outbox.at[h], send_sem.at[h]).wait()


def slot_targets(flagged, channel_owner):
    channel = jnp.arange(CHANNELS, dtype=jnp.int32)
    dropped = jnp.any(channel[:, None] == flagged[None, :], axis=1)
    kept_owner = jnp.where(dropped, -1, channel_owner)
    earlier = (kept_owner[None, :] == channel_owner[:, None]) & (channel[None, :] < channel[:, None])
    rank = jnp.sum(earlier.astype(jnp.int32), axis=1)
    return jnp.where(dropped, -1, channel_owner * CAPACITY + rank)


def on_device(voltages, filter_taps, flagged, channel_owner, ref_inputs):
    owners = lax.axis_size("inp")
    sections = lax.axis_size("sec")
    count = ref_inputs.shape[0]
    target = slot_targets(flagged, channel_owner).reshape(SHORT, RADIX)
    refs = jnp.full((REF_ROWS, 1), -1, jnp.int32).at[:count, 0].set(ref_inputs)
    high, low, twiddle = tables()
    inputs = owners * LOCAL // sections
    bf16, f32 = jnp.bfloat16, jnp.float32
    vmem = pl.BlockSpec(memory_space=pltpu.VMEM)
    return pl.pallas_call(
        functools.partial(kernel, owners, sections),
        out_shape=jax.ShapeDtypeStruct((1, CAPACITY, 2, count, inputs), f32),
        in_specs=[vmem] * 7,
        out_specs=vmem,
        scratch_shapes=[
            pltpu.VMEM((2, LOCAL, (TAPS - 1) * CHANNELS), bf16),
            pltpu.VMEM((RADIX * HALF * LOCAL, 2 * SHORT), bf16),
            pltpu.VMEM((RADIX * HALF * LOCAL, 2 * SHORT), bf16),
            pltpu.VMEM((2, 2 * HALF * LOCAL, CHANNELS), bf16),
            pltpu.VMEM((CHANNELS, owners * CAPACITY), bf16),
            pltpu.VMEM((2, owners, LOCAL, LANES), bf16),
            pltpu.VMEM((2, sections, inputs, LANES), bf16),
            pltpu.VMEM((2, sections * REF_ROWS, LANES), bf16),
            pltpu.VMEM((2, sections - 1, sections * REF_ROWS, LANES), bf16),
            pltpu.VMEM((CAPACITY * 2 * REF_ROWS, sections * LANES), bf16),
            pltpu.SemaphoreType.DMA((2,)),
            pltpu.SemaphoreType.DMA((2,)),
            pltpu.SemaphoreType.DMA((2,)),
            pltpu.SemaphoreType.DMA((2, sections - 1)),
            pltpu.SemaphoreType.DMA((2, sections - 1)),
        ],
        compiler_params=pltpu.CompilerParams(
            collective_id=0, has_side_effects=True, vmem_limit_bytes=48 * 1024 * 1024),
    )(voltages, filter_taps, target, refs, jnp.asarray(high), jnp.asarray(low), jnp.asarray(twiddle))


def solution(mesh):
    return jax.shard_map(
        on_device,
        mesh=mesh,
        in_specs=(P(None, "inp", "sec"), P(), P(), P(), P()),
        out_specs=P("inp", None, None, None, "sec"),
        check_vma=False,
    )
```

```python
import functools
import math

import jax
import jax.numpy as jnp
import numpy as np
from jax import lax
from jax.experimental import pallas as pl
from jax.experimental.pallas import tpu as pltpu
from jax.sharding import PartitionSpec as P

CHANNELS = 1024
TAPS = 4
RADIX = 4
SHORT = CHANNELS // RADIX
CAPACITY = 16
LOCAL = 16
HALF = 4
LANES = 128
GROUP = LANES // CAPACITY
REF_ROWS = 16
DEEP_ROWS = 24
CORES = 2
UNROLL = 8
MESH = pl.DeviceIdType.MESH


def tables():
    n = np.arange(SHORT)
    angle = 2.0 * math.pi * ((n[:, None] * n[None, :]) % SHORT) / SHORT
    cos, sin = np.cos(angle), np.sin(angle)
    full = np.block([[cos, -sin], [sin, cos]]) / math.sqrt(CHANNELS)
    high = full.astype(np.float32).astype(jnp.bfloat16)
    low = (full - high.astype(np.float64)).astype(np.float32).astype(jnp.bfloat16)
    turn = 2.0 * math.pi * np.arange(RADIX)[:, None] * n[None, :] / CHANNELS
    twiddle = np.stack([np.cos(turn), np.sin(turn)], axis=1).reshape(2 * RADIX, SHORT)
    return high, low, twiddle.astype(np.float32)


def kernel(owners, sections, volt_in, taps_in, flagged, owner_row, refs, high_in, low_in, twiddle_in, out,
           volt, taps, high, low, twiddle, column,
           halo, zhi, zlo, stage, onehot, outbox, inbox, refbox, refin, weights,
           load_sem, halo_sem, send_sem, recv_sem, ref_send, ref_recv):
    p, s = lax.axis_index("inp"), lax.axis_index("sec")
    span = owners // sections
    q = lax.div(p, span)
    place = lax.rem(p, span)
    row_count = owners // (GROUP * CORES)
    own_row = lax.div(p, GROUP * CORES)
    own_place = lax.rem(lax.div(p, CORES), GROUP)
    core = lax.rem(p, CORES)

    def holder(b, w, k):
        return (lax.rem(3 * k + b, row_count) * GROUP + k) * CORES + lax.rem(w + k, CORES)
    rows = span * LOCAL
    at_home = q == s

    loads = [
        pltpu.make_async_copy(here, there, load_sem.at[k]) for k, (here, there) in enumerate((
            (volt_in, volt), (taps_in, taps), (twiddle_in, twiddle), (high_in, high), (low_in, low)))]
    for load in loads:
        load.start()
    barrier = pltpu.get_barrier_semaphore()

    def greet(k, carry):
        for t in range(sections):
            pl.semaphore_signal(barrier, inc=1, device_id=(s * span + k, t), device_id_type=MESH)
        return carry
    lax.fori_loop(0, span, greet, 0, unroll=UNROLL)
    for d in range(1, sections):
        pl.semaphore_signal(barrier, inc=1, device_id=(p, lax.rem(s + d, sections)), device_id_type=MESH)

    lane = lax.broadcasted_iota(jnp.int32, (LOCAL, LANES), 1)
    block = lane // CAPACITY

    def spectra(h):
        for b in range(HALF):
            parts = []
            for part in range(2):
                pieces = []
                for n1 in range(RADIX):
                    total = None
                    for t in range(TAPS):
                        frame = h * HALF + b + t
                        if frame < 2 * HALF:
                            source = volt[part, :, pl.ds(frame * CHANNELS + n1 * SHORT, SHORT)].astype(jnp.float32)
                        else:
                            source = halo[part, :, pl.ds((frame - 2 * HALF) * CHANNELS + n1 * SHORT, SHORT)].astype(jnp.float32)
                            source = jnp.where(s == sections - 1, 0.0, source)
                        term = taps[t:t + 1, n1 * SHORT:(n1 + 1) * SHORT] * source
                        total = term if total is None else total + term
                    pieces.append(total)
                parts.append(pieces)
            (r0, r1, r2, r3), (i0, i1, i2, i3) = parts
            ar, ai, br, bi = r0 + r2, i0 + i2, r0 - r2, i0 - i2
            cr, ci, dr, di = r1 + r3, i1 + i3, r1 - r3, i1 - i3
            mixed = [(ar + cr, ai + ci), (br + di, bi - dr), (ar - cr, ai - ci), (br - di, bi + dr)]
            for c1 in range(RADIX):
                re, im = mixed[c1]
                if c1:
                    cos, sin = twiddle[2 * c1:2 * c1 + 1, :], twiddle[2 * c1 + 1:2 * c1 + 2, :]
                    re, im = re * cos + im * sin, im * cos - re * sin
                at = pl.ds((c1 * HALF + b) * LOCAL, LOCAL)
                for k, value in enumerate((re, im)):
                    top = value.astype(jnp.bfloat16)
                    zhi[at, k * SHORT:(k + 1) * SHORT] = top
                    zlo[at, k * SHORT:(k + 1) * SHORT] = (value - top.astype(jnp.float32)).astype(jnp.bfloat16)
        top = zhi[...]
        product = jnp.dot(top, high[...], preferred_element_type=jnp.float32)
        product += jnp.dot(zlo[...], high[...], preferred_element_type=jnp.float32)
        product += jnp.dot(top, low[...], preferred_element_type=jnp.float32)
        product = product.astype(jnp.bfloat16)
        deep = HALF * LOCAL
        for c1 in range(RADIX):
            for part in range(2):
                stage[h, part * deep:(part + 1) * deep, c1 * SHORT:(c1 + 1) * SHORT] = (
                    product[c1 * deep:(c1 + 1) * deep, part * SHORT:(part + 1) * SHORT])

    def place_channels():
        channel = lax.broadcasted_iota(jnp.int32, (1, CHANNELS), 1)
        dropped = channel == flagged[0]
        for k in range(1, flagged.shape[0]):
            dropped = dropped | (channel == flagged[k])
        kept = jnp.where(dropped, -1, owner_row[...]).astype(jnp.float32)
        upper = (lax.broadcasted_iota(jnp.int32, (LANES, LANES), 1)
                 < lax.broadcasted_iota(jnp.int32, (LANES, LANES), 0))
        ones = jnp.ones((LANES, LANES), jnp.bfloat16)
        for a in range(CHANNELS // LANES):
            across = jnp.broadcast_to(kept[:, a * LANES:(a + 1) * LANES], (LANES, LANES))
            own = across.T
            same = jnp.where(upper & (own == across), 1.0, 0.0)
            for e in range(a):
                same += jnp.where(own == kept[:, e * LANES:(e + 1) * LANES], 1.0, 0.0)
            rank = jnp.dot(same.astype(jnp.bfloat16), ones, preferred_element_type=jnp.float32)
            column[a * LANES:(a + 1) * LANES, :] = jnp.where(own < 0.0, -1.0, own * CAPACITY + rank).astype(jnp.int32)

    def build(j, carry):
        base = pl.multiple_of(j * LANES, LANES)
        spot = lax.broadcasted_iota(jnp.int32, (SHORT, LANES), 1)
        slot = holder(lax.div(j, CORES), lax.rem(j, CORES), spot // CAPACITY) * CAPACITY + spot % CAPACITY
        for c1 in range(RADIX):
            hit = column[pl.ds(c1, SHORT, stride=RADIX), :] == slot
            onehot[c1 * SHORT:(c1 + 1) * SHORT, pl.ds(base, LANES)] = jnp.where(hit, 1.0, 0.0).astype(jnp.bfloat16)
        return carry

    def parcel_of(o):
        k = lax.rem(lax.div(o, CORES), GROUP)
        w = lax.rem(lax.rem(o, CORES) + k, CORES)
        b = lax.rem(lax.div(o, CORES * GROUP) + 5 * k, row_count)
        return (b * CORES + w) * GROUP + k

    def around(d, size):
        return min(d % size, size - d % size)

    def far_first():
        landing = inbox.at[1, s, pl.ds(pl.multiple_of(place * LOCAL, LOCAL), LOCAL), :]
        steps = sorted(
            ((dy, dz, dc) for dc in range(CORES) for dy in range(row_count) for dz in range(GROUP)),
            key=lambda d: (-around(d[0], row_count) - around(d[1], GROUP), d[2], d[1], d[0]))
        flip_y = 1 - 2 * lax.rem(s, 2)
        flip_z = 1 - 2 * lax.rem(lax.div(s, 2), 2)
        for dy, dz, dc in steps:
            there_y = lax.rem(own_row + flip_y * dy + row_count, row_count)
            there_z = lax.rem(own_place + flip_z * dz + GROUP, GROUP)
            o = (there_y * GROUP + there_z) * CORES + lax.rem(core + dc, CORES)
            parcel = outbox.at[1, parcel_of(o)]

            def away():
                pltpu.make_async_remote_copy(
                    src_ref=parcel, dst_ref=landing, send_sem=send_sem.at[1],
                    recv_sem=recv_sem.at[1], device_id=(o, q), device_id_type=MESH).start()

            def home():
                pltpu.make_async_copy(parcel, landing, recv_sem.at[1]).start()

            if dy or dz or dc:
                away()
            else:
                pl.when(at_home)(home)
                pl.when(jnp.logical_not(at_home))(away)

    def ship(h):
        landing = inbox.at[h, s, pl.ds(pl.multiple_of(place * LOCAL, LOCAL), LOCAL), :]

        def one_batch(step, carry):
            b = lax.rem(own_row + 5 * own_place + 2 * s + step, row_count)
            base = pl.multiple_of(b * CORES * LANES, CORES * LANES)
            picked = jnp.dot(stage[h], onehot[:, pl.ds(base, CORES * LANES)], preferred_element_type=jnp.float32)
            for w in range(CORES):
                tiles = []
                for k in range(GROUP):
                    tile = picked[k * LOCAL:(k + 1) * LOCAL, w * LANES:(w + 1) * LANES]
                    tiles.append(pltpu.roll(tile, k * CAPACITY, 1) if k else tile)
                for bit in range(3):
                    reach = 1 << bit
                    taken = ((block // reach) % 2) == 1
                    tiles = [jnp.where(taken, tiles[(m + reach) % GROUP], tiles[m]) for m in range(GROUP)]
                for k in range(GROUP):
                    outbox[h, (b * CORES + w) * GROUP + k] = tiles[(GROUP - k) % GROUP].astype(jnp.bfloat16)

            for n in range(CORES * GROUP if h == 0 else 0):
                k = lax.rem(own_place + 1 + n, GROUP)
                w = lax.rem(core + n // GROUP, CORES)
                o = holder(b, w, k)
                parcel = outbox.at[h, (b * CORES + w) * GROUP + k]

                def away():
                    pltpu.make_async_remote_copy(
                        src_ref=parcel, dst_ref=landing, send_sem=send_sem.at[h],
                        recv_sem=recv_sem.at[h], device_id=(o, q), device_id_type=MESH).start()

                def home():
                    pltpu.make_async_copy(parcel, landing, recv_sem.at[h]).start()

                if (1 + n) % GROUP:
                    away()
                else:
                    mine = (o == p) & at_home
                    pl.when(mine)(home)
                    pl.when(jnp.logical_not(mine))(away)
            return carry
        lax.fori_loop(0, row_count, one_batch, 0)
        if h == 1:
            far_first()

    place_channels()
    lax.fori_loop(0, row_count * CORES, build, 0)
    for load in loads:
        load.wait()
    spectra(0)

    pl.semaphore_wait(barrier, owners + sections - 1)

    halo_copy = pltpu.make_async_remote_copy(
        src_ref=volt.at[:, :, pl.ds(0, (TAPS - 1) * CHANNELS)], dst_ref=halo, send_sem=halo_sem.at[0],
        recv_sem=halo_sem.at[1], device_id=(p, lax.rem(s + sections - 1, sections)), device_id_type=MESH)
    halo_copy.start()
    ship(0)
    halo_copy.wait()
    spectra(1)
    ship(1)

    index = lax.broadcasted_iota(jnp.int32, (REF_ROWS, rows), 1) + s * rows
    line = lax.broadcasted_iota(jnp.int32, (REF_ROWS, rows), 0)
    wanted = jnp.full((REF_ROWS, rows), -1, jnp.int32)
    for k in range(refs.shape[0]):
        wanted = jnp.where(line == k, refs[k], wanted)
    chosen = jnp.where(wanted == index, 1.0, 0.0).astype(jnp.bfloat16)

    def gather_refs(h):
        pltpu.make_async_copy(inbox.at[h], inbox.at[h], recv_sem.at[h]).wait()
        for t in range(sections):
            found = jnp.dot(chosen, inbox[h, t], preferred_element_type=jnp.float32)
            refbox[h, t * REF_ROWS:(t + 1) * REF_ROWS, :] = found.astype(jnp.bfloat16)
        copies = []
        for d in range(1, sections):
            copies.append(pltpu.make_async_remote_copy(
                src_ref=refbox.at[h], dst_ref=refin.at[h, d - 1], send_sem=ref_send.at[h, d - 1],
                recv_sem=ref_recv.at[h, d - 1], device_id=(p, lax.rem(s + d, sections)), device_id_type=MESH))
        for copy in copies:
            copy.start()
        return copies

    wide = lax.broadcasted_iota(jnp.int32, (DEEP_ROWS, LANES), 1)
    inner = wide % CAPACITY
    part_of = ((wide // CAPACITY + (GROUP - own_place)) % GROUP) // HALF
    sign = jnp.where(part_of == 1, 1.0, -1.0)
    straight = lax.broadcasted_iota(jnp.int32, (DEEP_ROWS, LANES), 0) % 2 == 0
    spread = jnp.where(
        lax.broadcasted_iota(jnp.int32, (DEEP_ROWS, REF_ROWS), 0) // 2
        == lax.broadcasted_iota(jnp.int32, (DEEP_ROWS, REF_ROWS), 1), 1.0, 0.0).astype(jnp.bfloat16)

    def correlate(h, copies):
        for copy in copies:
            copy.wait()
        pieces, sides = [], []
        for t in range(sections):
            at = pl.ds(t * REF_ROWS, REF_ROWS)
            found = refbox[h, at, :].astype(jnp.float32)
            for d in range(1, sections):
                found += refin[h, d - 1, at, :].astype(jnp.float32)
            pair = jnp.dot(spread, found.astype(jnp.bfloat16), preferred_element_type=jnp.float32)
            both = jnp.where(straight, pair, pltpu.roll(pair, LANES // 2, 1) * sign)
            masked = [jnp.where(inner == k, both, 0.0) for k in range(CAPACITY)]
            pieces.append(jnp.concatenate(masked, axis=0).astype(jnp.bfloat16))
            sides.append(inbox[h, t])
        return lax.dot_general(jnp.concatenate(pieces, axis=1), jnp.concatenate(sides, axis=1),
                               (((1,), (1,)), ((), ())), preferred_element_type=jnp.float32)

    tiles = rows // LANES
    first = gather_refs(0)
    total = correlate(0, first)
    for t in range(tiles):
        weights[t] = total[:, t * LANES:(t + 1) * LANES]
    second = gather_refs(1)
    total = correlate(1, second)
    for t in range(tiles):
        weights[t] = (weights[t] + total[:, t * LANES:(t + 1) * LANES]) * (1.0 / (2 * HALF * sections))
    count = refs.shape[0]
    for k in range(CAPACITY):
        for part in range(2):
            for t in range(tiles):
                start = k * count * tiles * 2 + 2 * t + part
                out[pl.ds(start, count, stride=2 * tiles), :] = weights[
                    t, pl.ds(k * DEEP_ROWS + part, count, stride=2), :]

    for h in range(2):
        @pl.when(at_home)
        def _():
            some = outbox.at[h, pl.ds(0, owners - 1)]
            pltpu.make_async_copy(some, some, send_sem.at[h]).wait()

        @pl.when(jnp.logical_not(at_home))
        def _():
            pltpu.make_async_copy(outbox.at[h], outbox.at[h], send_sem.at[h]).wait()


def on_device(voltages, filter_taps, flagged, channel_owner, ref_inputs):
    owners = lax.axis_size("inp")
    sections = lax.axis_size("sec")
    count = ref_inputs.shape[0]
    high, low, twiddle = tables()
    inputs = owners * LOCAL // sections
    bf16, f32 = jnp.bfloat16, jnp.float32
    vmem = pl.BlockSpec(memory_space=pltpu.VMEM)
    smem = pl.BlockSpec(memory_space=pltpu.SMEM)
    far = pl.BlockSpec(memory_space=pl.ANY)
    flat = pl.pallas_call(
        functools.partial(kernel, owners, sections),
        out_shape=jax.ShapeDtypeStruct((CAPACITY * count * 2 * inputs // LANES, LANES), f32),
        in_specs=[far, far, smem, vmem, smem, far, far, far],
        out_specs=vmem,
        scratch_shapes=[
            pltpu.VMEM(voltages.shape, bf16),
            pltpu.VMEM(filter_taps.shape, f32),
            pltpu.VMEM(high.shape, bf16),
            pltpu.VMEM(low.shape, bf16),
            pltpu.VMEM(twiddle.shape, f32),
            pltpu.VMEM((CHANNELS, LANES), jnp.int32),
            pltpu.VMEM((2, LOCAL, (TAPS - 1) * CHANNELS), bf16),
            pltpu.VMEM((RADIX * HALF * LOCAL, 2 * SHORT), bf16),
            pltpu.VMEM((RADIX * HALF * LOCAL, 2 * SHORT), bf16),
            pltpu.VMEM((2, 2 * HALF * LOCAL, CHANNELS), bf16),
            pltpu.VMEM((CHANNELS, owners * CAPACITY), bf16),
            pltpu.VMEM((2, owners, LOCAL, LANES), bf16),
            pltpu.VMEM((2, sections, inputs, LANES), bf16),
            pltpu.VMEM((2, sections * REF_ROWS, LANES), bf16),
            pltpu.VMEM((2, sections - 1, sections * REF_ROWS, LANES), bf16),
            pltpu.VMEM((inputs // LANES, CAPACITY * DEEP_ROWS, LANES), f32),
            pltpu.SemaphoreType.DMA((5,)),
            pltpu.SemaphoreType.DMA((2,)),
            pltpu.SemaphoreType.DMA((2,)),
            pltpu.SemaphoreType.DMA((2,)),
            pltpu.SemaphoreType.DMA((2, sections - 1)),
            pltpu.SemaphoreType.DMA((2, sections - 1)),
        ],
        compiler_params=pltpu.CompilerParams(
            collective_id=0, has_side_effects=True, vmem_limit_bytes=60 * 1024 * 1024),
    )(voltages, filter_taps, flagged, channel_owner.reshape(1, CHANNELS), ref_inputs,
      jnp.asarray(high), jnp.asarray(low), jnp.asarray(twiddle))
    split = flat.reshape(1, CAPACITY, count, inputs // LANES, 2, LANES)
    return split.transpose(0, 1, 4, 2, 3, 5).reshape(1, CAPACITY, 2, count, inputs)


def solution(mesh):
    return jax.shard_map(
        on_device,
        mesh=mesh,
        in_specs=(P(None, "inp", "sec"), P(), P(), P(), P()),
        out_specs=P("inp", None, None, None, "sec"),
        check_vma=False,
    )
```

```python
import functools
import math

import jax
import jax.numpy as jnp
import numpy as np
from jax import lax
from jax.experimental import pallas as pl
from jax.experimental.pallas import tpu as pltpu
from jax.sharding import PartitionSpec as P

CHANNELS = 1024
TAPS = 4
RADIX = 4
SHORT = CHANNELS // RADIX
CAPACITY = 16
LOCAL = 16
HALF = 4
LANES = 128
GROUP = LANES // CAPACITY
REF_ROWS = 16
CORES = 2
UNROLL = 8
SAVES = 2
MESH = pl.DeviceIdType.MESH


def tables():
    n = np.arange(SHORT)
    angle = 2.0 * math.pi * ((n[:, None] * n[None, :]) % SHORT) / SHORT
    cos, sin = np.cos(angle), np.sin(angle)
    full = np.block([[cos, -sin], [sin, cos]]) / math.sqrt(CHANNELS)
    high = full.astype(np.float32).astype(jnp.bfloat16)
    low = (full - high.astype(np.float64)).astype(np.float32).astype(jnp.bfloat16)
    turn = 2.0 * math.pi * np.arange(RADIX)[:, None] * n[None, :] / CHANNELS
    twiddle = np.stack([np.cos(turn), np.sin(turn)], axis=1).reshape(2 * RADIX, SHORT)
    return high, low, twiddle.astype(np.float32)


def kernel(owners, sections, volt_in, taps_in, flagged, owner_row, refs, high_in, low_in, twiddle_in, inbox_out, refs_out,
           volt, taps, high, low, twiddle, column,
           halo, zhi, zlo, stage, onehot, outbox, inbox, refbox,
           load_sem, save_sem, halo_sem, send_sem, recv_sem, ref_send, ref_recv):
    p, s = lax.axis_index("inp"), lax.axis_index("sec")
    span = owners // sections
    q = lax.div(p, span)
    place = lax.rem(p, span)
    row_count = owners // (GROUP * CORES)
    own_row = lax.div(p, GROUP * CORES)
    own_place = lax.rem(lax.div(p, CORES), GROUP)
    core = lax.rem(p, CORES)

    def holder(b, w, k):
        return (lax.rem(3 * k + b, row_count) * GROUP + k) * CORES + lax.rem(w + k, CORES)
    rows = span * LOCAL
    at_home = q == s

    loads = [
        pltpu.make_async_copy(here, there, load_sem.at[k]) for k, (here, there) in enumerate((
            (volt_in, volt), (taps_in, taps), (twiddle_in, twiddle), (high_in, high), (low_in, low)))]
    for load in loads:
        load.start()
    barrier = pltpu.get_barrier_semaphore()

    def greet(k, carry):
        for t in range(sections):
            pl.semaphore_signal(barrier, inc=1, device_id=(s * span + k, t), device_id_type=MESH)
        return carry
    lax.fori_loop(0, span, greet, 0, unroll=UNROLL)
    for d in range(1, sections):
        pl.semaphore_signal(barrier, inc=1, device_id=(p, lax.rem(s + d, sections)), device_id_type=MESH)

    lane = lax.broadcasted_iota(jnp.int32, (LOCAL, LANES), 1)
    block = lane // CAPACITY

    def spectra(h):
        for b in range(HALF):
            parts = []
            for part in range(2):
                pieces = []
                for n1 in range(RADIX):
                    total = None
                    for t in range(TAPS):
                        frame = h * HALF + b + t
                        if frame < 2 * HALF:
                            source = volt[part, :, pl.ds(frame * CHANNELS + n1 * SHORT, SHORT)].astype(jnp.float32)
                        else:
                            source = halo[part, :, pl.ds((frame - 2 * HALF) * CHANNELS + n1 * SHORT, SHORT)].astype(jnp.float32)
                            source = jnp.where(s == sections - 1, 0.0, source)
                        term = taps[t:t + 1, n1 * SHORT:(n1 + 1) * SHORT] * source
                        total = term if total is None else total + term
                    pieces.append(total)
                parts.append(pieces)
            (r0, r1, r2, r3), (i0, i1, i2, i3) = parts
            ar, ai, br, bi = r0 + r2, i0 + i2, r0 - r2, i0 - i2
            cr, ci, dr, di = r1 + r3, i1 + i3, r1 - r3, i1 - i3
            mixed = [(ar + cr, ai + ci), (br + di, bi - dr), (ar - cr, ai - ci), (br - di, bi + dr)]
            for c1 in range(RADIX):
                re, im = mixed[c1]
                if c1:
                    cos, sin = twiddle[2 * c1:2 * c1 + 1, :], twiddle[2 * c1 + 1:2 * c1 + 2, :]
                    re, im = re * cos + im * sin, im * cos - re * sin
                at = pl.ds((c1 * HALF + b) * LOCAL, LOCAL)
                for k, value in enumerate((re, im)):
                    top = value.astype(jnp.bfloat16)
                    zhi[at, k * SHORT:(k + 1) * SHORT] = top
                    zlo[at, k * SHORT:(k + 1) * SHORT] = (value - top.astype(jnp.float32)).astype(jnp.bfloat16)
        top = zhi[...]
        product = jnp.dot(top, high[...], preferred_element_type=jnp.float32)
        product += jnp.dot(zlo[...], high[...], preferred_element_type=jnp.float32)
        product += jnp.dot(top, low[...], preferred_element_type=jnp.float32)
        product = product.astype(jnp.bfloat16)
        deep = HALF * LOCAL
        for c1 in range(RADIX):
            for part in range(2):
                stage[h, part * deep:(part + 1) * deep, c1 * SHORT:(c1 + 1) * SHORT] = (
                    product[c1 * deep:(c1 + 1) * deep, part * SHORT:(part + 1) * SHORT])

    def place_channels():
        channel = lax.broadcasted_iota(jnp.int32, (1, CHANNELS), 1)
        dropped = channel == flagged[0]
        for k in range(1, flagged.shape[0]):
            dropped = dropped | (channel == flagged[k])
        kept = jnp.where(dropped, -1, owner_row[...]).astype(jnp.float32)
        upper = (lax.broadcasted_iota(jnp.int32, (LANES, LANES), 1)
                 < lax.broadcasted_iota(jnp.int32, (LANES, LANES), 0))
        ones = jnp.ones((LANES, LANES), jnp.bfloat16)
        for a in range(CHANNELS // LANES):
            across = jnp.broadcast_to(kept[:, a * LANES:(a + 1) * LANES], (LANES, LANES))
            own = across.T
            same = jnp.where(upper & (own == across), 1.0, 0.0)
            for e in range(a):
                same += jnp.where(own == kept[:, e * LANES:(e + 1) * LANES], 1.0, 0.0)
            rank = jnp.dot(same.astype(jnp.bfloat16), ones, preferred_element_type=jnp.float32)
            column[a * LANES:(a + 1) * LANES, :] = jnp.where(own < 0.0, -1.0, own * CAPACITY + rank).astype(jnp.int32)

    def build(j, carry):
        base = pl.multiple_of(j * LANES, LANES)
        spot = lax.broadcasted_iota(jnp.int32, (SHORT, LANES), 1)
        slot = holder(lax.div(j, CORES), lax.rem(j, CORES), spot // CAPACITY) * CAPACITY + spot % CAPACITY
        for c1 in range(RADIX):
            hit = column[pl.ds(c1, SHORT, stride=RADIX), :] == slot
            onehot[c1 * SHORT:(c1 + 1) * SHORT, pl.ds(base, LANES)] = jnp.where(hit, 1.0, 0.0).astype(jnp.bfloat16)
        return carry

    def parcel_of(o):
        k = lax.rem(lax.div(o, CORES), GROUP)
        w = lax.rem(lax.rem(o, CORES) + k, CORES)
        b = lax.rem(lax.div(o, CORES * GROUP) + 5 * k, row_count)
        return (b * CORES + w) * GROUP + k

    def around(d, size):
        return min(d % size, size - d % size)

    def far_first():
        landing = inbox.at[1, s, pl.ds(pl.multiple_of(place * LOCAL, LOCAL), LOCAL), :]
        steps = sorted(
            ((dy, dz, dc) for dc in range(CORES) for dy in range(row_count) for dz in range(GROUP)),
            key=lambda d: (-around(d[0], row_count) - around(d[1], GROUP), d[2], d[1], d[0]))
        flip_y = 1 - 2 * lax.rem(s, 2)
        flip_z = 1 - 2 * lax.rem(lax.div(s, 2), 2)
        for dy, dz, dc in steps:
            there_y = lax.rem(own_row + flip_y * dy + row_count, row_count)
            there_z = lax.rem(own_place + flip_z * dz + GROUP, GROUP)
            o = (there_y * GROUP + there_z) * CORES + lax.rem(core + dc, CORES)
            parcel = outbox.at[1, parcel_of(o)]

            def away():
                pltpu.make_async_remote_copy(
                    src_ref=parcel, dst_ref=landing, send_sem=send_sem.at[1],
                    recv_sem=recv_sem.at[1], device_id=(o, q), device_id_type=MESH).start()

            def home():
                pltpu.make_async_copy(parcel, landing, recv_sem.at[1]).start()

            if dy or dz or dc:
                away()
            else:
                pl.when(at_home)(home)
                pl.when(jnp.logical_not(at_home))(away)

    def ship(h):
        landing = inbox.at[h, s, pl.ds(pl.multiple_of(place * LOCAL, LOCAL), LOCAL), :]

        def one_batch(step, carry):
            b = lax.rem(own_row + 5 * own_place + 2 * s + step, row_count)
            base = pl.multiple_of(b * CORES * LANES, CORES * LANES)
            picked = jnp.dot(stage[h], onehot[:, pl.ds(base, CORES * LANES)], preferred_element_type=jnp.float32)
            for w in range(CORES):
                tiles = []
                for k in range(GROUP):
                    tile = picked[k * LOCAL:(k + 1) * LOCAL, w * LANES:(w + 1) * LANES]
                    tiles.append(pltpu.roll(tile, k * CAPACITY, 1) if k else tile)
                for bit in range(3):
                    reach = 1 << bit
                    taken = ((block // reach) % 2) == 1
                    tiles = [jnp.where(taken, tiles[(m + reach) % GROUP], tiles[m]) for m in range(GROUP)]
                for k in range(GROUP):
                    outbox[h, (b * CORES + w) * GROUP + k] = tiles[(GROUP - k) % GROUP].astype(jnp.bfloat16)

            for n in range(CORES * GROUP if h == 0 else 0):
                k = lax.rem(own_place + 1 + n, GROUP)
                w = lax.rem(core + n // GROUP, CORES)
                o = holder(b, w, k)
                parcel = outbox.at[h, (b * CORES + w) * GROUP + k]

                def away():
                    pltpu.make_async_remote_copy(
                        src_ref=parcel, dst_ref=landing, send_sem=send_sem.at[h],
                        recv_sem=recv_sem.at[h], device_id=(o, q), device_id_type=MESH).start()

                def home():
                    pltpu.make_async_copy(parcel, landing, recv_sem.at[h]).start()

                if (1 + n) % GROUP:
                    away()
                else:
                    mine = (o == p) & at_home
                    pl.when(mine)(home)
                    pl.when(jnp.logical_not(mine))(away)
            return carry
        lax.fori_loop(0, row_count, one_batch, 0)
        if h == 1:
            far_first()

    place_channels()
    lax.fori_loop(0, row_count * CORES, build, 0)
    for load in loads:
        load.wait()
    spectra(0)

    pl.semaphore_wait(barrier, owners + sections - 1)

    halo_copy = pltpu.make_async_remote_copy(
        src_ref=volt.at[:, :, pl.ds(0, (TAPS - 1) * CHANNELS)], dst_ref=halo, send_sem=halo_sem.at[0],
        recv_sem=halo_sem.at[1], device_id=(p, lax.rem(s + sections - 1, sections)), device_id_type=MESH)
    halo_copy.start()
    ship(0)
    halo_copy.wait()
    spectra(1)
    ship(1)

    index = lax.broadcasted_iota(jnp.int32, (REF_ROWS, rows), 1) + s * rows
    line = lax.broadcasted_iota(jnp.int32, (REF_ROWS, rows), 0)
    wanted = jnp.full((REF_ROWS, rows), -1, jnp.int32)
    for k in range(refs.shape[0]):
        wanted = jnp.where(line == k, refs[k], wanted)
    chosen = jnp.where(wanted == index, 1.0, 0.0).astype(jnp.bfloat16)

    def gather_refs(h):
        pltpu.make_async_copy(inbox.at[h], inbox.at[h], recv_sem.at[h]).wait()
        side = jnp.concatenate([inbox[h, t] for t in range(sections)], axis=1)
        refbox[h] = jnp.dot(chosen, side, preferred_element_type=jnp.float32).astype(jnp.bfloat16)
        copies = []
        for d in range(1, sections):
            copies.append(pltpu.make_async_remote_copy(
                src_ref=refbox.at[h], dst_ref=refs_out.at[h, d], send_sem=ref_send.at[h, d - 1],
                recv_sem=ref_recv.at[h, d - 1], device_id=(p, lax.rem(s + d, sections)), device_id_type=MESH))
        copies.append(pltpu.make_async_copy(refbox.at[h], refs_out.at[h, 0], save_sem.at[2 + h]))
        for copy in copies:
            copy.start()
        copies.append(pltpu.make_async_copy(inbox.at[h], inbox_out.at[h], save_sem.at[h]))
        copies[-1].start()
        return copies

    copies = [gather_refs(0), gather_refs(1)]
    for h in range(2):
        for copy in copies[h]:
            copy.wait()

    for h in range(2):
        @pl.when(at_home)
        def _():
            some = outbox.at[h, pl.ds(0, owners - 1)]
            pltpu.make_async_copy(some, some, send_sem.at[h]).wait()

        @pl.when(jnp.logical_not(at_home))
        def _():
            pltpu.make_async_copy(outbox.at[h], outbox.at[h], send_sem.at[h]).wait()


def correlate(sections, count, found_in, inbox_in, out_far, found, inbox, out, load_sem, save_sem):
    p = lax.axis_index("inp")
    place = lax.rem(lax.div(p, CORES), GROUP)
    loads = [pltpu.make_async_copy(found_in, found, load_sem.at[2])]
    loads += [pltpu.make_async_copy(inbox_in.at[h], inbox.at[h], load_sem.at[h]) for h in range(2)]
    for load in loads:
        load.start()
    lane = lax.broadcasted_iota(jnp.int32, (REF_ROWS, LANES), 1)
    part_of = ((lane // CAPACITY + (GROUP - place)) % GROUP) // HALF
    sign = jnp.where(part_of == 1, 1.0, -1.0)
    height = count * 2 * CAPACITY
    line = lax.broadcasted_iota(jnp.int32, (height, 2 * REF_ROWS), 0)
    some = CAPACITY // SAVES
    source = lax.rem(lax.div(line, 2 * some), count) + REF_ROWS * lax.rem(lax.div(line, some), 2)
    spread = jnp.where(source == lax.broadcasted_iota(jnp.int32, (height, 2 * REF_ROWS), 1), 1.0, 0.0)
    spread = spread.astype(jnp.bfloat16)
    loads[0].wait()
    pieces = []
    for h in range(2):
        total = found[h, 0].astype(jnp.float32)
        for d in range(1, sections):
            total += found[h, d].astype(jnp.float32)
        turned = [pltpu.roll(total[:, t * LANES:(t + 1) * LANES], LANES // 2, 1) * sign for t in range(sections)]
        pieces.append(jnp.concatenate([total, jnp.concatenate(turned, axis=1)], axis=0).astype(jnp.bfloat16))
    both = jnp.concatenate(pieces, axis=1)
    weights = jnp.dot(spread, both, preferred_element_type=jnp.float32)
    line = lax.broadcasted_iota(jnp.int32, weights.shape, 0)
    slot = lax.rem(line, some) + some * lax.div(line, 2 * count * some)
    keep = slot == lax.broadcasted_iota(jnp.int32, weights.shape, 1) % CAPACITY
    weights = jnp.where(keep, weights, 0.0).astype(jnp.bfloat16)
    for load in loads[1:]:
        load.wait()
    side = jnp.concatenate([inbox[h, t] for h in range(2) for t in range(sections)], axis=1)
    tiles = side.shape[0] // LANES
    saves = []
    share = 2 * count * some
    deep = 2 * count * tiles
    product = lax.dot_general(weights, side, (((1,), (1,)), ((), ())), preferred_element_type=jnp.float32)
    product = product * (1.0 / (2 * HALF * sections))
    for a in range(SAVES):
        total = product[a * share:(a + 1) * share, :]
        for r in range(count):
            for part in range(2):
                piece = total[(2 * r + part) * some:(2 * r + part + 1) * some, :]
                for t in range(tiles):
                    out[pl.ds(a * some * deep + (r * tiles + t) * 2 + part, some, stride=deep), :] = (
                        piece[:, t * LANES:(t + 1) * LANES])
        at = pl.ds(a * some * deep, some * deep)
        saves.append(pltpu.make_async_copy(out.at[at], out_far.at[at], save_sem.at[a]))
        saves[-1].start()
    for save in saves:
        save.wait()


def finish(sections, count, inputs, found, arrived):
    bf16, f32 = jnp.bfloat16, jnp.float32
    far = pl.BlockSpec(memory_space=pl.ANY)
    height = CAPACITY * count * 2 * inputs // LANES
    return pl.pallas_call(
        functools.partial(correlate, sections, count),
        out_shape=jax.ShapeDtypeStruct((height, LANES), f32),
        in_specs=[far, far],
        out_specs=far,
        scratch_shapes=[
            pltpu.VMEM(found.shape, bf16),
            pltpu.VMEM(arrived.shape, bf16),
            pltpu.VMEM((height, LANES), f32),
            pltpu.SemaphoreType.DMA((3,)),
            pltpu.SemaphoreType.DMA((SAVES,)),
        ],
        compiler_params=pltpu.CompilerParams(vmem_limit_bytes=60 * 1024 * 1024),
    )(found, arrived)


def on_device(voltages, filter_taps, flagged, channel_owner, ref_inputs):
    owners = lax.axis_size("inp")
    sections = lax.axis_size("sec")
    count = ref_inputs.shape[0]
    high, low, twiddle = tables()
    inputs = owners * LOCAL // sections
    bf16, f32 = jnp.bfloat16, jnp.float32
    vmem = pl.BlockSpec(memory_space=pltpu.VMEM)
    smem = pl.BlockSpec(memory_space=pltpu.SMEM)
    far = pl.BlockSpec(memory_space=pl.ANY)
    arrived, found = pl.pallas_call(
        functools.partial(kernel, owners, sections),
        out_shape=(
            jax.ShapeDtypeStruct((2, sections, inputs, LANES), bf16),
            jax.ShapeDtypeStruct((2, sections, REF_ROWS, sections * LANES), bf16),
        ),
        in_specs=[far, far, smem, vmem, smem, far, far, far],
        out_specs=(far, far),
        scratch_shapes=[
            pltpu.VMEM(voltages.shape, bf16),
            pltpu.VMEM(filter_taps.shape, f32),
            pltpu.VMEM(high.shape, bf16),
            pltpu.VMEM(low.shape, bf16),
            pltpu.VMEM(twiddle.shape, f32),
            pltpu.VMEM((CHANNELS, LANES), jnp.int32),
            pltpu.VMEM((2, LOCAL, (TAPS - 1) * CHANNELS), bf16),
            pltpu.VMEM((RADIX * HALF * LOCAL, 2 * SHORT), bf16),
            pltpu.VMEM((RADIX * HALF * LOCAL, 2 * SHORT), bf16),
            pltpu.VMEM((2, 2 * HALF * LOCAL, CHANNELS), bf16),
            pltpu.VMEM((CHANNELS, owners * CAPACITY), bf16),
            pltpu.VMEM((2, owners, LOCAL, LANES), bf16),
            pltpu.VMEM((2, sections, inputs, LANES), bf16),
            pltpu.VMEM((2, REF_ROWS, sections * LANES), bf16),
            pltpu.SemaphoreType.DMA((5,)),
            pltpu.SemaphoreType.DMA((4,)),
            pltpu.SemaphoreType.DMA((2,)),
            pltpu.SemaphoreType.DMA((2,)),
            pltpu.SemaphoreType.DMA((2,)),
            pltpu.SemaphoreType.DMA((2, sections - 1)),
            pltpu.SemaphoreType.DMA((2, sections - 1)),
        ],
        compiler_params=pltpu.CompilerParams(
            collective_id=0, has_side_effects=True, vmem_limit_bytes=60 * 1024 * 1024),
    )(voltages, filter_taps, flagged, channel_owner.reshape(1, CHANNELS), ref_inputs,
      jnp.asarray(high), jnp.asarray(low), jnp.asarray(twiddle))
    flat = finish(sections, count, inputs, found, arrived)
    split = flat.reshape(1, CAPACITY, count, inputs // LANES, 2, LANES)
    return split.transpose(0, 1, 4, 2, 3, 5).reshape(1, CAPACITY, 2, count, inputs)


def solution(mesh):
    return jax.shard_map(
        on_device,
        mesh=mesh,
        in_specs=(P(None, "inp", "sec"), P(), P(), P(), P()),
        out_specs=P("inp", None, None, None, "sec"),
        check_vma=False,
    )
```

```python
import functools
import math

import jax
import jax.numpy as jnp
import numpy as np
from jax import lax
from jax.experimental import pallas as pl
from jax.experimental.pallas import tpu as pltpu
from jax.sharding import PartitionSpec as P

CHANNELS = 1024
TAPS = 4
RADIX = 4
SHORT = CHANNELS // RADIX
CAPACITY = 16
LOCAL = 16
HALF = 4
LANES = 128
GROUP = LANES // CAPACITY
REF_ROWS = 16
CORES = 2
UNROLL = 8
SAVES = 2
MESH = pl.DeviceIdType.MESH


def tables():
    n = np.arange(SHORT)
    angle = 2.0 * math.pi * ((n[:, None] * n[None, :]) % SHORT) / SHORT
    cos, sin = np.cos(angle), np.sin(angle)
    full = np.block([[cos, -sin], [sin, cos]]) / math.sqrt(CHANNELS)
    high = full.astype(np.float32).astype(jnp.bfloat16)
    low = (full - high.astype(np.float64)).astype(np.float32).astype(jnp.bfloat16)
    turn = 2.0 * math.pi * np.arange(RADIX)[:, None] * n[None, :] / CHANNELS
    twiddle = np.stack([np.cos(turn), np.sin(turn)], axis=1).reshape(2 * RADIX, SHORT)
    return high, low, twiddle.astype(np.float32)


def kernel(owners, sections, volt_in, taps_in, flagged_in, owner_in, refs_in, high_in, low_in, twiddle_in, inbox_out, refs_out,
           volt, taps, flagged, owner_row, refs, high, low, twiddle, column,
           halo, zhi, zlo, stage, onehot, outbox, inbox, refbox,
           load_sem, save_sem, halo_sem, send_sem, recv_sem, ref_send, ref_recv):
    p, s = lax.axis_index("inp"), lax.axis_index("sec")
    span = owners // sections
    q = lax.div(p, span)
    place = lax.rem(p, span)
    row_count = owners // (GROUP * CORES)
    own_row = lax.div(p, GROUP * CORES)
    own_place = lax.rem(lax.div(p, CORES), GROUP)
    core = lax.rem(p, CORES)

    def holder(b, w, k):
        return (lax.rem(3 * k + b, row_count) * GROUP + k) * CORES + lax.rem(w + k, CORES)
    rows = span * LOCAL
    at_home = q == s

    loads = [
        pltpu.make_async_copy(here, there, load_sem.at[k]) for k, (here, there) in enumerate((
            (flagged_in, flagged), (owner_in, owner_row), (refs_in, refs), (volt_in, volt), (taps_in, taps),
            (twiddle_in, twiddle), (high_in, high), (low_in, low)))]
    for load in loads:
        load.start()
    barrier = pltpu.get_barrier_semaphore()

    def greet(k, carry):
        for t in range(sections):
            pl.semaphore_signal(barrier, inc=1, device_id=(s * span + k, t), device_id_type=MESH)
        return carry
    lax.fori_loop(0, span, greet, 0, unroll=UNROLL)
    for d in range(1, sections):
        pl.semaphore_signal(barrier, inc=1, device_id=(p, lax.rem(s + d, sections)), device_id_type=MESH)

    lane = lax.broadcasted_iota(jnp.int32, (LOCAL, LANES), 1)
    block = lane // CAPACITY

    def spectra(h):
        for b in range(HALF):
            parts = []
            for part in range(2):
                pieces = []
                for n1 in range(RADIX):
                    total = None
                    for t in range(TAPS):
                        frame = h * HALF + b + t
                        if frame < 2 * HALF:
                            source = volt[part, :, pl.ds(frame * CHANNELS + n1 * SHORT, SHORT)].astype(jnp.float32)
                        else:
                            source = halo[part, :, pl.ds((frame - 2 * HALF) * CHANNELS + n1 * SHORT, SHORT)].astype(jnp.float32)
                            source = jnp.where(s == sections - 1, 0.0, source)
                        term = taps[t:t + 1, n1 * SHORT:(n1 + 1) * SHORT] * source
                        total = term if total is None else total + term
                    pieces.append(total)
                parts.append(pieces)
            (r0, r1, r2, r3), (i0, i1, i2, i3) = parts
            ar, ai, br, bi = r0 + r2, i0 + i2, r0 - r2, i0 - i2
            cr, ci, dr, di = r1 + r3, i1 + i3, r1 - r3, i1 - i3
            mixed = [(ar + cr, ai + ci), (br + di, bi - dr), (ar - cr, ai - ci), (br - di, bi + dr)]
            for c1 in range(RADIX):
                re, im = mixed[c1]
                if c1:
                    cos, sin = twiddle[2 * c1:2 * c1 + 1, :], twiddle[2 * c1 + 1:2 * c1 + 2, :]
                    re, im = re * cos + im * sin, im * cos - re * sin
                at = pl.ds((c1 * HALF + b) * LOCAL, LOCAL)
                for k, value in enumerate((re, im)):
                    top = value.astype(jnp.bfloat16)
                    zhi[at, k * SHORT:(k + 1) * SHORT] = top
                    zlo[at, k * SHORT:(k + 1) * SHORT] = (value - top.astype(jnp.float32)).astype(jnp.bfloat16)
        top = zhi[...]
        product = jnp.dot(top, high[...], preferred_element_type=jnp.float32)
        product += jnp.dot(zlo[...], high[...], preferred_element_type=jnp.float32)
        product += jnp.dot(top, low[...], preferred_element_type=jnp.float32)
        product = product.astype(jnp.bfloat16)
        deep = HALF * LOCAL
        for c1 in range(RADIX):
            for part in range(2):
                stage[h, part * deep:(part + 1) * deep, c1 * SHORT:(c1 + 1) * SHORT] = (
                    product[c1 * deep:(c1 + 1) * deep, part * SHORT:(part + 1) * SHORT])

    def place_channels():
        channel = lax.broadcasted_iota(jnp.int32, (1, CHANNELS), 1)
        dropped = channel == flagged[0]
        for k in range(1, flagged.shape[0]):
            dropped = dropped | (channel == flagged[k])
        kept = jnp.where(dropped, -1, owner_row[...]).astype(jnp.float32)
        upper = (lax.broadcasted_iota(jnp.int32, (LANES, LANES), 1)
                 < lax.broadcasted_iota(jnp.int32, (LANES, LANES), 0))
        ones = jnp.ones((LANES, LANES), jnp.bfloat16)
        for a in range(CHANNELS // LANES):
            across = jnp.broadcast_to(kept[:, a * LANES:(a + 1) * LANES], (LANES, LANES))
            own = across.T
            same = jnp.where(upper & (own == across), 1.0, 0.0)
            for e in range(a):
                same += jnp.where(own == kept[:, e * LANES:(e + 1) * LANES], 1.0, 0.0)
            rank = jnp.dot(same.astype(jnp.bfloat16), ones, preferred_element_type=jnp.float32)
            column[a * LANES:(a + 1) * LANES, :] = jnp.where(own < 0.0, -1.0, own * CAPACITY + rank).astype(jnp.int32)

    def build(j, carry):
        base = pl.multiple_of(j * LANES, LANES)
        spot = lax.broadcasted_iota(jnp.int32, (SHORT, LANES), 1)
        slot = holder(lax.div(j, CORES), lax.rem(j, CORES), spot // CAPACITY) * CAPACITY + spot % CAPACITY
        for c1 in range(RADIX):
            hit = column[pl.ds(c1, SHORT, stride=RADIX), :] == slot
            onehot[c1 * SHORT:(c1 + 1) * SHORT, pl.ds(base, LANES)] = jnp.where(hit, 1.0, 0.0).astype(jnp.bfloat16)
        return carry

    def parcel_of(o):
        k = lax.rem(lax.div(o, CORES), GROUP)
        w = lax.rem(lax.rem(o, CORES) + k, CORES)
        b = lax.rem(lax.div(o, CORES * GROUP) + 5 * k, row_count)
        return (b * CORES + w) * GROUP + k

    def around(d, size):
        return min(d % size, size - d % size)

    def far_first():
        landing = inbox.at[1, s, pl.ds(pl.multiple_of(place * LOCAL, LOCAL), LOCAL), :]
        steps = sorted(
            ((dy, dz, dc) for dc in range(CORES) for dy in range(row_count) for dz in range(GROUP)),
            key=lambda d: (-around(d[0], row_count) - around(d[1], GROUP), d[2], d[1], d[0]))
        flip_y = 1 - 2 * lax.rem(s, 2)
        flip_z = 1 - 2 * lax.rem(lax.div(s, 2), 2)
        for dy, dz, dc in steps:
            there_y = lax.rem(own_row + flip_y * dy + row_count, row_count)
            there_z = lax.rem(own_place + flip_z * dz + GROUP, GROUP)
            o = (there_y * GROUP + there_z) * CORES + lax.rem(core + dc, CORES)
            parcel = outbox.at[1, parcel_of(o)]

            def away():
                pltpu.make_async_remote_copy(
                    src_ref=parcel, dst_ref=landing, send_sem=send_sem.at[1],
                    recv_sem=recv_sem.at[1], device_id=(o, q), device_id_type=MESH).start()

            def home():
                pltpu.make_async_copy(parcel, landing, recv_sem.at[1]).start()

            if dy or dz or dc:
                away()
            else:
                pl.when(at_home)(home)
                pl.when(jnp.logical_not(at_home))(away)

    def ship(h):
        landing = inbox.at[h, s, pl.ds(pl.multiple_of(place * LOCAL, LOCAL), LOCAL), :]

        def one_batch(step, carry):
            b = lax.rem(own_row + 5 * own_place + 2 * s + step, row_count)
            base = pl.multiple_of(b * CORES * LANES, CORES * LANES)
            picked = jnp.dot(stage[h], onehot[:, pl.ds(base, CORES * LANES)], preferred_element_type=jnp.float32)
            for w in range(CORES):
                tiles = []
                for k in range(GROUP):
                    tile = picked[k * LOCAL:(k + 1) * LOCAL, w * LANES:(w + 1) * LANES]
                    tiles.append(pltpu.roll(tile, k * CAPACITY, 1) if k else tile)
                for bit in range(3):
                    reach = 1 << bit
                    taken = ((block // reach) % 2) == 1
                    tiles = [jnp.where(taken, tiles[(m + reach) % GROUP], tiles[m]) for m in range(GROUP)]
                for k in range(GROUP):
                    outbox[h, (b * CORES + w) * GROUP + k] = tiles[(GROUP - k) % GROUP].astype(jnp.bfloat16)

            for n in range(CORES * GROUP if h == 0 else 0):
                k = lax.rem(own_place + 1 + n, GROUP)
                w = lax.rem(core + n // GROUP, CORES)
                o = holder(b, w, k)
                parcel = outbox.at[h, (b * CORES + w) * GROUP + k]

                def away():
                    pltpu.make_async_remote_copy(
                        src_ref=parcel, dst_ref=landing, send_sem=send_sem.at[h],
                        recv_sem=recv_sem.at[h], device_id=(o, q), device_id_type=MESH).start()

                def home():
                    pltpu.make_async_copy(parcel, landing, recv_sem.at[h]).start()

                if (1 + n) % GROUP:
                    away()
                else:
                    mine = (o == p) & at_home
                    pl.when(mine)(home)
                    pl.when(jnp.logical_not(mine))(away)
            return carry
        lax.fori_loop(0, row_count, one_batch, 0)
        if h == 1:
            far_first()

    for load in loads[:3]:
        load.wait()
    place_channels()
    lax.fori_loop(0, row_count * CORES, build, 0)
    for load in loads[3:]:
        load.wait()
    spectra(0)

    pl.semaphore_wait(barrier, owners + sections - 1)

    halo_copy = pltpu.make_async_remote_copy(
        src_ref=volt.at[:, :, pl.ds(0, (TAPS - 1) * CHANNELS)], dst_ref=halo, send_sem=halo_sem.at[0],
        recv_sem=halo_sem.at[1], device_id=(p, lax.rem(s + sections - 1, sections)), device_id_type=MESH)
    halo_copy.start()
    ship(0)
    halo_copy.wait()
    spectra(1)
    ship(1)

    index = lax.broadcasted_iota(jnp.int32, (REF_ROWS, rows), 1) + s * rows
    line = lax.broadcasted_iota(jnp.int32, (REF_ROWS, rows), 0)
    wanted = jnp.full((REF_ROWS, rows), -1, jnp.int32)
    for k in range(refs.shape[0]):
        wanted = jnp.where(line == k, refs[k], wanted)
    chosen = jnp.where(wanted == index, 1.0, 0.0).astype(jnp.bfloat16)

    def gather_refs(h):
        pltpu.make_async_copy(inbox.at[h], inbox.at[h], recv_sem.at[h]).wait()
        side = jnp.concatenate([inbox[h, t] for t in range(sections)], axis=1)
        refbox[h] = jnp.dot(chosen, side, preferred_element_type=jnp.float32).astype(jnp.bfloat16)
        copies = []
        for d in range(1, sections):
            copies.append(pltpu.make_async_remote_copy(
                src_ref=refbox.at[h], dst_ref=refs_out.at[h, d], send_sem=ref_send.at[h, d - 1],
                recv_sem=ref_recv.at[h, d - 1], device_id=(p, lax.rem(s + d, sections)), device_id_type=MESH))
        copies.append(pltpu.make_async_copy(refbox.at[h], refs_out.at[h, 0], save_sem.at[2 + h]))
        for copy in copies:
            copy.start()
        copies.append(pltpu.make_async_copy(inbox.at[h], inbox_out.at[h], save_sem.at[h]))
        copies[-1].start()
        return copies

    copies = [gather_refs(0), gather_refs(1)]
    for h in range(2):
        for copy in copies[h]:
            copy.wait()

    for h in range(2):
        @pl.when(at_home)
        def _():
            some = outbox.at[h, pl.ds(0, owners - 1)]
            pltpu.make_async_copy(some, some, send_sem.at[h]).wait()

        @pl.when(jnp.logical_not(at_home))
        def _():
            pltpu.make_async_copy(outbox.at[h], outbox.at[h], send_sem.at[h]).wait()


def correlate(sections, count, found_in, inbox_in, out_far, found, inbox, out, load_sem, save_sem):
    p = lax.axis_index("inp")
    place = lax.rem(lax.div(p, CORES), GROUP)
    loads = [pltpu.make_async_copy(found_in, found, load_sem.at[2])]
    loads += [pltpu.make_async_copy(inbox_in.at[h], inbox.at[h], load_sem.at[h]) for h in range(2)]
    for load in loads:
        load.start()
    lane = lax.broadcasted_iota(jnp.int32, (REF_ROWS, LANES), 1)
    part_of = ((lane // CAPACITY + (GROUP - place)) % GROUP) // HALF
    sign = jnp.where(part_of == 1, 1.0, -1.0)
    height = count * 2 * CAPACITY
    line = lax.broadcasted_iota(jnp.int32, (height, 2 * REF_ROWS), 0)
    some = CAPACITY // SAVES
    source = lax.rem(lax.div(line, 2 * some), count) + REF_ROWS * lax.rem(lax.div(line, some), 2)
    spread = jnp.where(source == lax.broadcasted_iota(jnp.int32, (height, 2 * REF_ROWS), 1), 1.0, 0.0)
    spread = spread.astype(jnp.bfloat16)
    loads[0].wait()
    pieces = []
    for h in range(2):
        total = found[h, 0].astype(jnp.float32)
        for d in range(1, sections):
            total += found[h, d].astype(jnp.float32)
        turned = [pltpu.roll(total[:, t * LANES:(t + 1) * LANES], LANES // 2, 1) * sign for t in range(sections)]
        pieces.append(jnp.concatenate([total, jnp.concatenate(turned, axis=1)], axis=0).astype(jnp.bfloat16))
    both = jnp.concatenate(pieces, axis=1)
    weights = jnp.dot(spread, both, preferred_element_type=jnp.float32)
    line = lax.broadcasted_iota(jnp.int32, weights.shape, 0)
    slot = lax.rem(line, some) + some * lax.div(line, 2 * count * some)
    keep = slot == lax.broadcasted_iota(jnp.int32, weights.shape, 1) % CAPACITY
    weights = jnp.where(keep, weights, 0.0).astype(jnp.bfloat16)
    for load in loads[1:]:
        load.wait()
    side = jnp.concatenate([inbox[h, t] for h in range(2) for t in range(sections)], axis=1)
    tiles = side.shape[0] // LANES
    saves = []
    share = 2 * count * some
    deep = 2 * count * tiles
    product = lax.dot_general(weights, side, (((1,), (1,)), ((), ())), preferred_element_type=jnp.float32)
    product = product * (1.0 / (2 * HALF * sections))
    for a in range(SAVES):
        total = product[a * share:(a + 1) * share, :]
        for r in range(count):
            for part in range(2):
                piece = total[(2 * r + part) * some:(2 * r + part + 1) * some, :]
                for t in range(tiles):
                    out[pl.ds(a * some * deep + (r * tiles + t) * 2 + part, some, stride=deep), :] = (
                        piece[:, t * LANES:(t + 1) * LANES])
        at = pl.ds(a * some * deep, some * deep)
        saves.append(pltpu.make_async_copy(out.at[at], out_far.at[at], save_sem.at[a]))
        saves[-1].start()
    for save in saves:
        save.wait()


def finish(sections, count, inputs, found, arrived):
    bf16, f32 = jnp.bfloat16, jnp.float32
    far = pl.BlockSpec(memory_space=pl.ANY)
    height = CAPACITY * count * 2 * inputs // LANES
    return pl.pallas_call(
        functools.partial(correlate, sections, count),
        out_shape=jax.ShapeDtypeStruct((height, LANES), f32),
        in_specs=[far, far],
        out_specs=far,
        scratch_shapes=[
            pltpu.VMEM(found.shape, bf16),
            pltpu.VMEM(arrived.shape, bf16),
            pltpu.VMEM((height, LANES), f32),
            pltpu.SemaphoreType.DMA((3,)),
            pltpu.SemaphoreType.DMA((SAVES,)),
        ],
        compiler_params=pltpu.CompilerParams(vmem_limit_bytes=60 * 1024 * 1024),
    )(found, arrived)


def on_device(voltages, filter_taps, flagged, channel_owner, ref_inputs):
    owners = lax.axis_size("inp")
    sections = lax.axis_size("sec")
    count = ref_inputs.shape[0]
    high, low, twiddle = tables()
    inputs = owners * LOCAL // sections
    bf16, f32 = jnp.bfloat16, jnp.float32
    far = pl.BlockSpec(memory_space=pl.ANY)
    arrived, found = pl.pallas_call(
        functools.partial(kernel, owners, sections),
        out_shape=(
            jax.ShapeDtypeStruct((2, sections, inputs, LANES), bf16),
            jax.ShapeDtypeStruct((2, sections, REF_ROWS, sections * LANES), bf16),
        ),
        in_specs=[far] * 8,
        out_specs=(far, far),
        scratch_shapes=[
            pltpu.VMEM(voltages.shape, bf16),
            pltpu.VMEM(filter_taps.shape, f32),
            pltpu.SMEM(flagged.shape, jnp.int32),
            pltpu.VMEM((1, CHANNELS), jnp.int32),
            pltpu.SMEM(ref_inputs.shape, jnp.int32),
            pltpu.VMEM(high.shape, bf16),
            pltpu.VMEM(low.shape, bf16),
            pltpu.VMEM(twiddle.shape, f32),
            pltpu.VMEM((CHANNELS, LANES), jnp.int32),
            pltpu.VMEM((2, LOCAL, (TAPS - 1) * CHANNELS), bf16),
            pltpu.VMEM((RADIX * HALF * LOCAL, 2 * SHORT), bf16),
            pltpu.VMEM((RADIX * HALF * LOCAL, 2 * SHORT), bf16),
            pltpu.VMEM((2, 2 * HALF * LOCAL, CHANNELS), bf16),
            pltpu.VMEM((CHANNELS, owners * CAPACITY), bf16),
            pltpu.VMEM((2, owners, LOCAL, LANES), bf16),
            pltpu.VMEM((2, sections, inputs, LANES), bf16),
            pltpu.VMEM((2, REF_ROWS, sections * LANES), bf16),
            pltpu.SemaphoreType.DMA((8,)),
            pltpu.SemaphoreType.DMA((4,)),
            pltpu.SemaphoreType.DMA((2,)),
            pltpu.SemaphoreType.DMA((2,)),
            pltpu.SemaphoreType.DMA((2,)),
            pltpu.SemaphoreType.DMA((2, sections - 1)),
            pltpu.SemaphoreType.DMA((2, sections - 1)),
        ],
        compiler_params=pltpu.CompilerParams(
            collective_id=0, has_side_effects=True, vmem_limit_bytes=60 * 1024 * 1024),
    )(voltages, filter_taps, flagged, channel_owner.reshape(1, CHANNELS), ref_inputs,
      jnp.asarray(high), jnp.asarray(low), jnp.asarray(twiddle))
    flat = finish(sections, count, inputs, found, arrived)
    split = flat.reshape(1, CAPACITY, count, inputs // LANES, 2, LANES)
    return split.transpose(0, 1, 4, 2, 3, 5).reshape(1, CAPACITY, 2, count, inputs)


def solution(mesh):
    return jax.shard_map(
        on_device,
        mesh=mesh,
        in_specs=(P(None, "inp", "sec"), P(), P(), P(), P()),
        out_specs=P("inp", None, None, None, "sec"),
        check_vma=False,
    )
```

```python
import functools
import math

import jax
import jax.numpy as jnp
import numpy as np
from jax import lax
from jax.experimental import pallas as pl
from jax.experimental.pallas import tpu as pltpu
from jax.sharding import PartitionSpec as P

CHANNELS = 1024
TAPS = 4
RADIX = 4
SHORT = CHANNELS // RADIX
CAPACITY = 16
LOCAL = 16
HALF = 4
LANES = 128
GROUP = LANES // CAPACITY
REF_ROWS = 16
CORES = 2
UNROLL = 8
SAVES = 2
MESH = pl.DeviceIdType.MESH


def tables():
    n = np.arange(SHORT)
    angle = 2.0 * math.pi * ((n[:, None] * n[None, :]) % SHORT) / SHORT
    cos, sin = np.cos(angle), np.sin(angle)
    full = np.block([[cos, -sin], [sin, cos]]) / math.sqrt(CHANNELS)
    high = full.astype(np.float32).astype(jnp.bfloat16)
    low = (full - high.astype(np.float64)).astype(np.float32).astype(jnp.bfloat16)
    turn = 2.0 * math.pi * np.arange(RADIX)[:, None] * n[None, :] / CHANNELS
    twiddle = np.stack([np.cos(turn), np.sin(turn)], axis=1).reshape(2 * RADIX, SHORT)
    return high, low, twiddle.astype(np.float32)


def kernel(owners, sections, volt_in, taps_in, flagged_in, owner_in, refs_in, high_in, low_in, twiddle_in, inbox_out, refs_out, begun_out,
           volt, taps, flagged, owner_row, refs, high, low, twiddle, column,
           halo, zhi, zlo, stage, onehot, outbox, inbox, refbox, early, begun,
           load_sem, save_sem, halo_sem, send_sem, recv_sem, ref_send, ref_recv):
    p, s = lax.axis_index("inp"), lax.axis_index("sec")
    span = owners // sections
    q = lax.div(p, span)
    place = lax.rem(p, span)
    row_count = owners // (GROUP * CORES)
    own_row = lax.div(p, GROUP * CORES)
    own_place = lax.rem(lax.div(p, CORES), GROUP)
    core = lax.rem(p, CORES)

    def holder(b, w, k):
        return (lax.rem(3 * k + b, row_count) * GROUP + k) * CORES + lax.rem(w + k, CORES)
    rows = span * LOCAL
    at_home = q == s

    loads = [
        pltpu.make_async_copy(here, there, load_sem.at[k]) for k, (here, there) in enumerate((
            (flagged_in, flagged), (owner_in, owner_row), (refs_in, refs), (volt_in, volt), (taps_in, taps),
            (twiddle_in, twiddle), (high_in, high), (low_in, low)))]
    for load in loads:
        load.start()
    barrier = pltpu.get_barrier_semaphore()

    def greet(k, carry):
        for t in range(sections):
            pl.semaphore_signal(barrier, inc=1, device_id=(s * span + k, t), device_id_type=MESH)
        return carry
    lax.fori_loop(0, span, greet, 0, unroll=UNROLL)
    for d in range(1, sections):
        pl.semaphore_signal(barrier, inc=1, device_id=(p, lax.rem(s + d, sections)), device_id_type=MESH)

    lane = lax.broadcasted_iota(jnp.int32, (LOCAL, LANES), 1)
    block = lane // CAPACITY

    def spectra(h):
        for b in range(HALF):
            parts = []
            for part in range(2):
                pieces = []
                for n1 in range(RADIX):
                    total = None
                    for t in range(TAPS):
                        frame = h * HALF + b + t
                        if frame < 2 * HALF:
                            source = volt[part, :, pl.ds(frame * CHANNELS + n1 * SHORT, SHORT)].astype(jnp.float32)
                        else:
                            source = halo[part, :, pl.ds((frame - 2 * HALF) * CHANNELS + n1 * SHORT, SHORT)].astype(jnp.float32)
                            source = jnp.where(s == sections - 1, 0.0, source)
                        term = taps[t:t + 1, n1 * SHORT:(n1 + 1) * SHORT] * source
                        total = term if total is None else total + term
                    pieces.append(total)
                parts.append(pieces)
            (r0, r1, r2, r3), (i0, i1, i2, i3) = parts
            ar, ai, br, bi = r0 + r2, i0 + i2, r0 - r2, i0 - i2
            cr, ci, dr, di = r1 + r3, i1 + i3, r1 - r3, i1 - i3
            mixed = [(ar + cr, ai + ci), (br + di, bi - dr), (ar - cr, ai - ci), (br - di, bi + dr)]
            for c1 in range(RADIX):
                re, im = mixed[c1]
                if c1:
                    cos, sin = twiddle[2 * c1:2 * c1 + 1, :], twiddle[2 * c1 + 1:2 * c1 + 2, :]
                    re, im = re * cos + im * sin, im * cos - re * sin
                at = pl.ds((c1 * HALF + b) * LOCAL, LOCAL)
                for k, value in enumerate((re, im)):
                    top = value.astype(jnp.bfloat16)
                    zhi[at, k * SHORT:(k + 1) * SHORT] = top
                    zlo[at, k * SHORT:(k + 1) * SHORT] = (value - top.astype(jnp.float32)).astype(jnp.bfloat16)
        top = zhi[...]
        product = jnp.dot(top, high[...], preferred_element_type=jnp.float32)
        product += jnp.dot(zlo[...], high[...], preferred_element_type=jnp.float32)
        product += jnp.dot(top, low[...], preferred_element_type=jnp.float32)
        product = product.astype(jnp.bfloat16)
        deep = HALF * LOCAL
        for c1 in range(RADIX):
            for part in range(2):
                stage[h, part * deep:(part + 1) * deep, c1 * SHORT:(c1 + 1) * SHORT] = (
                    product[c1 * deep:(c1 + 1) * deep, part * SHORT:(part + 1) * SHORT])

    def place_channels():
        channel = lax.broadcasted_iota(jnp.int32, (1, CHANNELS), 1)
        dropped = channel == flagged[0]
        for k in range(1, flagged.shape[0]):
            dropped = dropped | (channel == flagged[k])
        kept = jnp.where(dropped, -1, owner_row[...]).astype(jnp.float32)
        upper = (lax.broadcasted_iota(jnp.int32, (LANES, LANES), 1)
                 < lax.broadcasted_iota(jnp.int32, (LANES, LANES), 0))
        ones = jnp.ones((LANES, LANES), jnp.bfloat16)
        for a in range(CHANNELS // LANES):
            across = jnp.broadcast_to(kept[:, a * LANES:(a + 1) * LANES], (LANES, LANES))
            own = across.T
            same = jnp.where(upper & (own == across), 1.0, 0.0)
            for e in range(a):
                same += jnp.where(own == kept[:, e * LANES:(e + 1) * LANES], 1.0, 0.0)
            rank = jnp.dot(same.astype(jnp.bfloat16), ones, preferred_element_type=jnp.float32)
            column[a * LANES:(a + 1) * LANES, :] = jnp.where(own < 0.0, -1.0, own * CAPACITY + rank).astype(jnp.int32)

    def build(j, carry):
        base = pl.multiple_of(j * LANES, LANES)
        spot = lax.broadcasted_iota(jnp.int32, (SHORT, LANES), 1)
        slot = holder(lax.div(j, CORES), lax.rem(j, CORES), spot // CAPACITY) * CAPACITY + spot % CAPACITY
        for c1 in range(RADIX):
            hit = column[pl.ds(c1, SHORT, stride=RADIX), :] == slot
            onehot[c1 * SHORT:(c1 + 1) * SHORT, pl.ds(base, LANES)] = jnp.where(hit, 1.0, 0.0).astype(jnp.bfloat16)
        return carry

    def parcel_of(o):
        k = lax.rem(lax.div(o, CORES), GROUP)
        w = lax.rem(lax.rem(o, CORES) + k, CORES)
        b = lax.rem(lax.div(o, CORES * GROUP) + 5 * k, row_count)
        return (b * CORES + w) * GROUP + k

    def around(d, size):
        return min(d % size, size - d % size)

    def far_first():
        landing = inbox.at[1, s, pl.ds(pl.multiple_of(place * LOCAL, LOCAL), LOCAL), :]
        steps = sorted(
            ((dy, dz, dc) for dc in range(CORES) for dy in range(row_count) for dz in range(GROUP)),
            key=lambda d: (-around(d[0], row_count) - around(d[1], GROUP), d[2], d[1], d[0]))
        flip_y = 1 - 2 * lax.rem(s, 2)
        flip_z = 1 - 2 * lax.rem(lax.div(s, 2), 2)
        for dy, dz, dc in steps:
            there_y = lax.rem(own_row + flip_y * dy + row_count, row_count)
            there_z = lax.rem(own_place + flip_z * dz + GROUP, GROUP)
            o = (there_y * GROUP + there_z) * CORES + lax.rem(core + dc, CORES)
            parcel = outbox.at[1, parcel_of(o)]

            def away():
                pltpu.make_async_remote_copy(
                    src_ref=parcel, dst_ref=landing, send_sem=send_sem.at[1],
                    recv_sem=recv_sem.at[1], device_id=(o, q), device_id_type=MESH).start()

            def home():
                pltpu.make_async_copy(parcel, landing, recv_sem.at[1]).start()

            if dy or dz or dc:
                away()
            else:
                pl.when(at_home)(home)
                pl.when(jnp.logical_not(at_home))(away)

    def ship(h):
        landing = inbox.at[h, s, pl.ds(pl.multiple_of(place * LOCAL, LOCAL), LOCAL), :]

        def one_batch(step, carry):
            b = lax.rem(own_row + 5 * own_place + 2 * s + step, row_count)
            base = pl.multiple_of(b * CORES * LANES, CORES * LANES)
            picked = jnp.dot(stage[h], onehot[:, pl.ds(base, CORES * LANES)], preferred_element_type=jnp.float32)
            for w in range(CORES):
                tiles = []
                for k in range(GROUP):
                    tile = picked[k * LOCAL:(k + 1) * LOCAL, w * LANES:(w + 1) * LANES]
                    tiles.append(pltpu.roll(tile, k * CAPACITY, 1) if k else tile)
                for bit in range(3):
                    reach = 1 << bit
                    taken = ((block // reach) % 2) == 1
                    tiles = [jnp.where(taken, tiles[(m + reach) % GROUP], tiles[m]) for m in range(GROUP)]
                for k in range(GROUP):
                    outbox[h, (b * CORES + w) * GROUP + k] = tiles[(GROUP - k) % GROUP].astype(jnp.bfloat16)

            for n in range(CORES * GROUP if h == 0 else 0):
                k = lax.rem(own_place + 1 + n, GROUP)
                w = lax.rem(core + n // GROUP, CORES)
                o = holder(b, w, k)
                parcel = outbox.at[h, (b * CORES + w) * GROUP + k]

                def away():
                    pltpu.make_async_remote_copy(
                        src_ref=parcel, dst_ref=landing, send_sem=send_sem.at[h],
                        recv_sem=recv_sem.at[h], device_id=(o, q), device_id_type=MESH).start()

                def home():
                    pltpu.make_async_copy(parcel, landing, recv_sem.at[h]).start()

                if (1 + n) % GROUP:
                    away()
                else:
                    mine = (o == p) & at_home
                    pl.when(mine)(home)
                    pl.when(jnp.logical_not(mine))(away)
            return carry
        lax.fori_loop(0, row_count, one_batch, 0)
        if h == 1:
            far_first()

    for load in loads[:3]:
        load.wait()
    place_channels()
    lax.fori_loop(0, row_count * CORES, build, 0)
    for load in loads[3:]:
        load.wait()
    spectra(0)

    pl.semaphore_wait(barrier, owners + sections - 1)

    halo_copy = pltpu.make_async_remote_copy(
        src_ref=volt.at[:, :, pl.ds(0, (TAPS - 1) * CHANNELS)], dst_ref=halo, send_sem=halo_sem.at[0],
        recv_sem=halo_sem.at[1], device_id=(p, lax.rem(s + sections - 1, sections)), device_id_type=MESH)
    halo_copy.start()
    ship(0)
    halo_copy.wait()
    spectra(1)
    ship(1)

    index = lax.broadcasted_iota(jnp.int32, (REF_ROWS, rows), 1) + s * rows
    line = lax.broadcasted_iota(jnp.int32, (REF_ROWS, rows), 0)
    wanted = jnp.full((REF_ROWS, rows), -1, jnp.int32)
    for k in range(refs.shape[0]):
        wanted = jnp.where(line == k, refs[k], wanted)
    chosen = jnp.where(wanted == index, 1.0, 0.0).astype(jnp.bfloat16)

    def gather_refs(h):
        pltpu.make_async_copy(inbox.at[h], inbox.at[h], recv_sem.at[h]).wait()
        side = jnp.concatenate([inbox[h, t] for t in range(sections)], axis=1)
        refbox[h] = jnp.dot(chosen, side, preferred_element_type=jnp.float32).astype(jnp.bfloat16)
        copies = []
        for d in range(1, sections):
            copies.append(pltpu.make_async_remote_copy(
                src_ref=refbox.at[h], dst_ref=refs_out.at[h, d], send_sem=ref_send.at[h, d - 1],
                recv_sem=ref_recv.at[h, d - 1], device_id=(p, lax.rem(s + d, sections)), device_id_type=MESH))
        copies.append(pltpu.make_async_copy(refbox.at[h], refs_out.at[h, 0], save_sem.at[2 + h]))
        for copy in copies:
            copy.start()
        if h == 1:
            copies.append(pltpu.make_async_copy(inbox.at[h], inbox_out, save_sem.at[0]))
            copies[-1].start()
        return copies

    for copy in gather_refs(0):
        copy.wait()
    fetch = pltpu.make_async_copy(refs_out.at[0], early, save_sem.at[1])
    fetch.start()
    fetch.wait()
    begun[...] = half_product(sections, refs.shape[0], own_place, early, lambda: [inbox[0, t] for t in range(sections)])
    keep_half = pltpu.make_async_copy(begun, begun_out, save_sem.at[4])
    keep_half.start()
    for copy in gather_refs(1):
        copy.wait()
    keep_half.wait()

    for h in range(2):
        @pl.when(at_home)
        def _():
            some = outbox.at[h, pl.ds(0, owners - 1)]
            pltpu.make_async_copy(some, some, send_sem.at[h]).wait()

        @pl.when(jnp.logical_not(at_home))
        def _():
            pltpu.make_async_copy(outbox.at[h], outbox.at[h], send_sem.at[h]).wait()


def half_product(sections, count, place, found, sides):
    lane = lax.broadcasted_iota(jnp.int32, (REF_ROWS, LANES), 1)
    part_of = ((lane // CAPACITY + (GROUP - place)) % GROUP) // HALF
    sign = jnp.where(part_of == 1, 1.0, -1.0)
    height = count * 2 * CAPACITY
    some = CAPACITY // SAVES
    line = lax.broadcasted_iota(jnp.int32, (height, 2 * REF_ROWS), 0)
    source = lax.rem(lax.div(line, 2 * some), count) + REF_ROWS * lax.rem(lax.div(line, some), 2)
    spread = jnp.where(source == lax.broadcasted_iota(jnp.int32, (height, 2 * REF_ROWS), 1), 1.0, 0.0)
    total = found[0].astype(jnp.float32)
    for d in range(1, sections):
        total += found[d].astype(jnp.float32)
    turned = [pltpu.roll(total[:, t * LANES:(t + 1) * LANES], LANES // 2, 1) * sign for t in range(sections)]
    both = jnp.concatenate([total, jnp.concatenate(turned, axis=1)], axis=0).astype(jnp.bfloat16)
    weights = jnp.dot(spread.astype(jnp.bfloat16), both, preferred_element_type=jnp.float32)
    line = lax.broadcasted_iota(jnp.int32, weights.shape, 0)
    slot = lax.rem(line, some) + some * lax.div(line, 2 * count * some)
    keep = slot == lax.broadcasted_iota(jnp.int32, weights.shape, 1) % CAPACITY
    weights = jnp.where(keep, weights, 0.0).astype(jnp.bfloat16)
    side = jnp.concatenate(sides(), axis=1)
    return lax.dot_general(weights, side, (((1,), (1,)), ((), ())), preferred_element_type=jnp.float32)


def correlate(sections, count, found_in, inbox_in, begun_in, out_far, found, inbox, begun, out, load_sem, save_sem):
    place = lax.rem(lax.div(lax.axis_index("inp"), CORES), GROUP)
    loads = [pltpu.make_async_copy(here, there, load_sem.at[k]) for k, (here, there) in enumerate((
        (found_in.at[1], found), (inbox_in, inbox), (begun_in, begun)))]
    for load in loads:
        load.start()
    loads[0].wait()

    def sides():
        loads[1].wait()
        return [inbox[t] for t in range(sections)]
    product = half_product(sections, count, place, found, sides)
    loads[2].wait()
    product = (product + begun[...]) * (1.0 / (2 * HALF * sections))
    tiles = inbox.shape[1] // LANES
    saves = []
    some = CAPACITY // SAVES
    share = 2 * count * some
    deep = 2 * count * tiles
    for a in range(SAVES):
        total = product[a * share:(a + 1) * share, :]
        for r in range(count):
            for part in range(2):
                piece = total[(2 * r + part) * some:(2 * r + part + 1) * some, :]
                for t in range(tiles):
                    out[pl.ds(a * some * deep + (r * tiles + t) * 2 + part, some, stride=deep), :] = (
                        piece[:, t * LANES:(t + 1) * LANES])
        at = pl.ds(a * some * deep, some * deep)
        saves.append(pltpu.make_async_copy(out.at[at], out_far.at[at], save_sem.at[a]))
        saves[-1].start()
    for save in saves:
        save.wait()


def finish(sections, count, inputs, found, arrived, begun):
    bf16, f32 = jnp.bfloat16, jnp.float32
    far = pl.BlockSpec(memory_space=pl.ANY)
    height = CAPACITY * count * 2 * inputs // LANES
    return pl.pallas_call(
        functools.partial(correlate, sections, count),
        out_shape=jax.ShapeDtypeStruct((height, LANES), f32),
        in_specs=[far] * 3,
        out_specs=far,
        scratch_shapes=[
            pltpu.VMEM(found.shape[1:], bf16),
            pltpu.VMEM(arrived.shape, bf16),
            pltpu.VMEM(begun.shape, f32),
            pltpu.VMEM((height, LANES), f32),
            pltpu.SemaphoreType.DMA((3,)),
            pltpu.SemaphoreType.DMA((SAVES,)),
        ],
        compiler_params=pltpu.CompilerParams(vmem_limit_bytes=60 * 1024 * 1024),
    )(found, arrived, begun)


def on_device(voltages, filter_taps, flagged, channel_owner, ref_inputs):
    owners = lax.axis_size("inp")
    sections = lax.axis_size("sec")
    count = ref_inputs.shape[0]
    high, low, twiddle = tables()
    inputs = owners * LOCAL // sections
    bf16, f32 = jnp.bfloat16, jnp.float32
    far = pl.BlockSpec(memory_space=pl.ANY)
    arrived, found, begun = pl.pallas_call(
        functools.partial(kernel, owners, sections),
        out_shape=(
            jax.ShapeDtypeStruct((sections, inputs, LANES), bf16),
            jax.ShapeDtypeStruct((2, sections, REF_ROWS, sections * LANES), bf16),
            jax.ShapeDtypeStruct((count * 2 * CAPACITY, inputs), f32),
        ),
        in_specs=[far] * 8,
        out_specs=(far, far, far),
        scratch_shapes=[
            pltpu.VMEM(voltages.shape, bf16),
            pltpu.VMEM(filter_taps.shape, f32),
            pltpu.SMEM(flagged.shape, jnp.int32),
            pltpu.VMEM((1, CHANNELS), jnp.int32),
            pltpu.SMEM(ref_inputs.shape, jnp.int32),
            pltpu.VMEM(high.shape, bf16),
            pltpu.VMEM(low.shape, bf16),
            pltpu.VMEM(twiddle.shape, f32),
            pltpu.VMEM((CHANNELS, LANES), jnp.int32),
            pltpu.VMEM((2, LOCAL, (TAPS - 1) * CHANNELS), bf16),
            pltpu.VMEM((RADIX * HALF * LOCAL, 2 * SHORT), bf16),
            pltpu.VMEM((RADIX * HALF * LOCAL, 2 * SHORT), bf16),
            pltpu.VMEM((2, 2 * HALF * LOCAL, CHANNELS), bf16),
            pltpu.VMEM((CHANNELS, owners * CAPACITY), bf16),
            pltpu.VMEM((2, owners, LOCAL, LANES), bf16),
            pltpu.VMEM((2, sections, inputs, LANES), bf16),
            pltpu.VMEM((2, REF_ROWS, sections * LANES), bf16),
            pltpu.VMEM((sections, REF_ROWS, sections * LANES), bf16),
            pltpu.VMEM((count * 2 * CAPACITY, inputs), f32),
            pltpu.SemaphoreType.DMA((8,)),
            pltpu.SemaphoreType.DMA((5,)),
            pltpu.SemaphoreType.DMA((2,)),
            pltpu.SemaphoreType.DMA((2,)),
            pltpu.SemaphoreType.DMA((2,)),
            pltpu.SemaphoreType.DMA((2, sections - 1)),
            pltpu.SemaphoreType.DMA((2, sections - 1)),
        ],
        compiler_params=pltpu.CompilerParams(
            collective_id=0, has_side_effects=True, vmem_limit_bytes=60 * 1024 * 1024),
    )(voltages, filter_taps, flagged, channel_owner.reshape(1, CHANNELS), ref_inputs,
      jnp.asarray(high), jnp.asarray(low), jnp.asarray(twiddle))
    flat = finish(sections, count, inputs, found, arrived, begun)
    split = flat.reshape(1, CAPACITY, count, inputs // LANES, 2, LANES)
    return split.transpose(0, 1, 4, 2, 3, 5).reshape(1, CAPACITY, 2, count, inputs)


def solution(mesh):
    return jax.shard_map(
        on_device,
        mesh=mesh,
        in_specs=(P(None, "inp", "sec"), P(), P(), P(), P()),
        out_specs=P("inp", None, None, None, "sec"),
        check_vma=False,
    )
```
